512 devices in a mesh: tm: 16 (over x, z_lo), clus: 32 (over z_hi, y, core).
Axes of the slice: x: 4, y: 8, z: 8 (z_hi: 2, z_lo: 4; z = z_hi * 4 + z_lo), core: 2. Of those that a mesh axis runs over, the one named last changes fastest.
Arguments:
- currents: bfloat16 [1024, 1024, 128], P('clus', 'tm'), may hold values from -6 to 6
- excitation: bfloat16 [1024, 1024, 128], P('clus', 'tm'), may hold values from -6 to 6
- neighbours: int32 [1024, 30], P('clus'), may hold values from -1 to 1023, as said below
- lag_profile: bfloat16 [30, 64], replicated, may hold values from -0.125 to 0.125
- couplings: bfloat16 [30, 128, 128], replicated, may hold values from -0.5 to 0.5
- block_inverses: bfloat16 [1024, 128, 128], P('clus'), may hold values from -0.5 to 0.5
- charge_map: bfloat16 [128, 128], replicated, may hold values from -0.015625 to 0.015625
- potential: bfloat16 [128, 128], replicated, may hold values from -0.5 to 0.5
Outputs:
- updated: bfloat16 [1024, 1024, 128], P('clus', 'tm')
- residual: float32 [1024, 1024, 128], P('clus', 'tm')
The draws below stay inside these ranges and needn't reach their ends.
Inputs may be any that keep to these rules, and one draw needn't show every extreme that they name: `neighbours`: row j lists distinct panel clusters from j // 32 * 32 - 32 to j // 32 * 32 + 2 * 32 - 1, modulo 1024; entries -1 pad the end of a row, and every row has a cluster in its first slot.
All inputs are finite; a program needn't handle non-finite values.
Results may differ from the reference program's by a relative error of at most 0.0051.
Values may be sent and summed in bfloat16 or wider, within the bound.
No kernel may reach another device: no remote copies, remote signals or barrier semaphores. Data moves between devices by JAX's collectives and lax.ppermute only.
A program may use at most 64 MiB of HBM per device.

```python
import jax
import jax.numpy as jnp
from jax import lax

B = 128
M = 128
NB = 30
LAG = 64
CPD = 32
TB = 64
CLUSTERS = 1024
STEPS = 1024
N_TM = 16


def draw_neighbours(key, part):
    candidates = 3 * CPD
    first_key, second_key = jax.random.split(jax.random.fold_in(key, 11))
    scores = jax.random.randint(first_key, (CLUSTERS, candidates), 0, 1 << 20) * candidates + jnp.arange(candidates)[None, :]
    order = jnp.argsort(scores, axis=1)
    taken = min(NB, candidates)
    chosen = order[:, :taken]
    device_first = (jnp.arange(CLUSTERS) // CPD - 1) * CPD
    cluster_ids = (device_first[:, None] + chosen) % CLUSTERS
    counts = jax.random.randint(second_key, (CLUSTERS,), taken - taken // 4, taken + 1)
    cluster_ids = jnp.where(jnp.arange(taken)[None, :] < counts[:, None], cluster_ids, -1)
    if taken < NB:
        cluster_ids = jnp.concatenate([cluster_ids, -jnp.ones((CLUSTERS, NB - taken), cluster_ids.dtype)], axis=1)
    return cluster_ids.astype(jnp.int32)


def steps_of(stream_key, extent, cuts, smallest, high):
    def one(position, shards_of):
        steps = jax.random.uniform(jax.random.fold_in(jax.random.fold_in(stream_key, 6), position), (shards_of,), jnp.float32, smallest / len(cuts), high / len(cuts))
        return jnp.repeat(jnp.exp(steps), extent[position] // shards_of).reshape((-1,) + (1,) * (len(extent) - position - 1))

    level = one(*cuts[0])
    for cut in cuts[1:]:
        level = level * one(*cut)
    return level


def centred(key, dims, scale, bound, cuts=(), held_as=jnp.bfloat16):
    factor_of = steps_of(key, dims, cuts, -0.22, 0.18) if cuts else 1.0
    array = jax.random.normal(key, dims, jnp.float32) * scale * factor_of
    return jnp.minimum(jnp.maximum(array, -bound), bound).astype(held_as)


def setup_inputs(seed: int = 0) -> dict:
    key_of = jax.random.split(jax.random.key(seed), 9)
    currents = centred(key_of[0], (CLUSTERS, STEPS, B), 1.0, 6.0, ((0, 32), (1, 16)))
    excitation = centred(key_of[1], (CLUSTERS, STEPS, B), 1.0, 6.0, ((0, 32), (1, 16)))
    neighbours = draw_neighbours(jax.random.fold_in(key_of[8], 71), 0)
    lag_profile = centred(key_of[3], (NB, LAG), (NB * LAG) ** -0.5, 0.125)
    couplings = centred(key_of[4], (NB, B, B), B ** -0.5, 0.5)
    block_inverses = centred(key_of[5], (CLUSTERS, B, B), B ** -0.5, 0.5, ((0, 32),))
    charge_map = centred(key_of[6], (B, M), (B * STEPS) ** -0.5, 0.015625)
    potential = centred(key_of[7], (M, B), M ** -0.5, 0.5)
    return dict(currents=currents, excitation=excitation, neighbours=neighbours, lag_profile=lag_profile, couplings=couplings, block_inverses=block_inverses, charge_map=charge_map, potential=potential)


def reference(currents, excitation, neighbours, lag_profile, couplings, block_inverses, charge_map, potential):
    clusters, steps, unknowns = currents.shape
    slot_count = lag_profile.shape[0]
    window = TB + LAG
    current32 = currents.astype(jnp.float32)
    padded = jnp.concatenate([jnp.zeros((clusters, LAG, unknowns), jnp.float32), current32], axis=1)
    present = neighbours >= 0
    safe_ids = jnp.where(present, neighbours, 0).astype(jnp.int32)
    present_f = present.astype(jnp.float32)
    lag_index = jnp.arange(TB)[:, None] + LAG - jnp.arange(window)[None, :]
    lag_onehot = (lag_index[:, :, None] == jnp.arange(LAG)[None, None, :]).astype(jnp.float32)
    toeplitz = jnp.einsum('kl,tsl->kts', lag_profile.astype(jnp.float32), lag_onehot)
    coupling = couplings.astype(jnp.float32)

    def block_field(block_index):
        start = (block_index * TB).astype(jnp.int32)
        window_slab = lax.dynamic_slice_in_dim(padded, start, window, axis=1)

        def slot_step(accum, slot):
            gathered = jnp.take(window_slab, safe_ids[:, slot], axis=0)
            filtered = jnp.einsum('ts,csb->ctb', toeplitz[slot], gathered) * present_f[:, slot][:, None, None]
            filtered = lax.optimization_barrier(filtered.astype(jnp.bfloat16)).astype(jnp.float32)
            return accum + jnp.einsum('ctb,bd->ctd', filtered, coupling[slot]), None

        start_field = jnp.zeros((clusters, TB, unknowns), jnp.float32)
        near_block, _ = lax.scan(slot_step, start_field, jnp.arange(slot_count).astype(jnp.int32))
        return near_block

    near_field = lax.map(block_field, jnp.arange(N_TM).astype(jnp.int32))
    near_field = jnp.transpose(near_field, (1, 0, 2, 3)).reshape(clusters, steps, unknowns)
    increments = jnp.dot(currents.reshape(-1, unknowns), charge_map, preferred_element_type=jnp.float32)
    increments = increments.reshape(clusters, steps, -1)
    charge = jnp.cumsum(increments, axis=1)
    charge_rounded = charge.astype(jnp.bfloat16)
    charge_field = jnp.dot(charge_rounded.reshape(clusters * steps, -1), potential, preferred_element_type=jnp.float32)
    charge_field = charge_field.reshape(clusters, steps, unknowns)
    residual = excitation.astype(jnp.float32) - near_field - charge_field
    residual_rounded = residual.astype(jnp.bfloat16)
    correction = jnp.einsum('ctb,cbd->ctd', residual_rounded.astype(jnp.float32), block_inverses.astype(jnp.float32))
    updated = (current32 + correction).astype(jnp.bfloat16)
    return updated, residual
```

```python
import jax
import jax.numpy as jnp
from jax import lax
from jax.experimental import pallas as pl
from jax.experimental.pallas import tpu as pltpu
from jax.sharding import PartitionSpec as P

F32, BF16 = jnp.float32, jnp.bfloat16
MIB = 1 << 20


def whole(space=pltpu.VMEM):
    return pl.BlockSpec(memory_space=space)


def dot(a, b):
    return jnp.dot(a, b, preferred_element_type=F32)


def charge_kernel(cur_ref, map_ref, running_ref, totals_ref):
    per_dev, steps, unknowns = cur_ref.shape
    row = lax.broadcasted_iota(jnp.int32, (steps, 2 * steps), 0)
    col = lax.broadcasted_iota(jnp.int32, (steps, 2 * steps), 1)
    lower = (row >= col % steps).astype(F32).astype(BF16)
    group = 8

    @pl.loop(0, per_dev // group)
    def _(g):
        first = g * group
        rows = cur_ref[pl.ds(first, group)].reshape(group * steps, unknowns)
        inc = dot(rows, map_ref[...])
        high = inc.astype(BF16)
        low = (inc - high.astype(F32)).astype(BF16)
        last = []
        for i in range(group):
            cut = slice(i * steps, (i + 1) * steps)
            run = dot(lower, jnp.concatenate([high[cut], low[cut]], axis=0))
            running_ref[first + i] = run
            last.append(run[steps - 1 : steps])
        totals_ref[pl.ds(first, group)] = jnp.concatenate(last, axis=0)


def near_kernel(
    ids_ref, edge_ref, lag_ref, coup_ref, own_ref, up_ref, down_ref, wrap_ref,
    head_ref, tail_ref, field, blocks, toep, terms, sems,
):
    per_dev, steps, unknowns = own_ref.shape
    slots = coup_ref.shape[0]
    group = 8

    own_copy = pltpu.make_async_copy(own_ref, field.at[pl.ds(per_dev, per_dev)], sems.at[0])
    own_copy.start()

    def fetch(ref, start, sem):
        return pltpu.make_async_copy(ref, field.at[pl.ds(start, per_dev)], sem)

    low_edge, high_edge = edge_ref[0] > 0, edge_ref[1] > 0

    @pl.when(low_edge)
    def _():
        fetch(wrap_ref, 0, sems.at[1]).start()

    @pl.when(jnp.logical_not(low_edge))
    def _():
        fetch(up_ref, 0, sems.at[1]).start()

    @pl.when(high_edge)
    def _():
        fetch(wrap_ref, 2 * per_dev, sems.at[2]).start()

    @pl.when(jnp.logical_not(high_edge))
    def _():
        fetch(down_ref, 2 * per_dev, sems.at[2]).start()

    field[3 * per_dev] = jnp.zeros((steps, unknowns), BF16)
    lane = lax.broadcasted_iota(jnp.int32, (2 * steps, 2 * steps), 1)
    for p in range(slots // 2):
        square = jnp.zeros((unknowns, unknowns), BF16)
        blocks[p, :unknowns, :unknowns] = coup_ref[2 * p]
        blocks[p, :unknowns, unknowns:] = square
        blocks[p, unknowns:, :unknowns] = square
        blocks[p, unknowns:, unknowns:] = coup_ref[2 * p + 1]
        even = jnp.broadcast_to(lag_ref[2 * p : 2 * p + 1, :], lane.shape)
        odd = jnp.broadcast_to(lag_ref[2 * p + 1 : 2 * p + 2, :], lane.shape)
        even = pltpu.roll(even, 0, 1, stride=1, stride_axis=0)
        odd = pltpu.roll(odd, steps, 1, stride=1, stride_axis=0)
        both = jnp.where(lane < steps, even, odd)
        toep[:, p * 2 * steps : (p + 1) * 2 * steps] = both.astype(BF16)
    own_copy.wait()
    fetch(up_ref, 0, sems.at[1]).wait()
    fetch(down_ref, 2 * per_dev, sems.at[2]).wait()

    @pl.loop(0, per_dev // group)
    def _(g):
        first = g * group
        for p in range(slots // 2):
            rows = [
                jnp.concatenate(
                    [
                        field[ids_ref[first + i, 2 * p]],
                        field[ids_ref[first + i, 2 * p + 1]],
                    ],
                    axis=1,
                )
                for i in range(group)
            ]
            z = dot(jnp.concatenate(rows, axis=0), blocks[p]).astype(BF16)
            for i in range(group):
                cut = slice(i * steps, (i + 1) * steps)
                lanes = slice((i % 2) * unknowns, (i % 2 + 1) * unknowns)
                for h in range(2):
                    at = (2 * p + h) * steps
                    terms[i // 2, at : at + steps, lanes] = z[cut, h * unknowns : (h + 1) * unknowns]
        for i in range(0, group, 2):
            out = dot(toep[...], terms[i // 2])
            for j in range(2):
                lanes = slice(j * unknowns, (j + 1) * unknowns)
                head_ref[first + i + j] = out[:steps, lanes]
                tail_ref[first + i + j] = out[steps:, lanes].astype(BF16)


def base_kernel(exc_ref, head_ref, running_ref, before_ref, pot_ref, base_ref):
    per_dev, steps, unknowns = exc_ref.shape
    group = 8

    @pl.loop(0, per_dev // group)
    def _(g):
        at = pl.ds(g * group, group)
        charge = (running_ref[at] + before_ref[at][:, None, :]).astype(BF16)
        field = dot(charge.reshape(group * steps, -1), pot_ref[...])
        field = field.reshape(group, steps, unknowns)
        base_ref[at] = exc_ref[at].astype(F32) - head_ref[at] - field


def final_kernel(cur_ref, base_ref, tail_ref, inv_ref, updated_ref, residual_ref):
    for i in range(cur_ref.shape[0]):
        residual = base_ref[i] - tail_ref[i].astype(F32)
        residual_ref[i] = residual
        correction = dot(residual.astype(BF16), inv_ref[i])
        updated_ref[i] = (cur_ref[i].astype(F32) + correction).astype(BF16)


def on_device(
    currents, excitation, neighbours, lag_profile, couplings, block_inverses, charge_map, potential
):
    per_dev, steps, unknowns = currents.shape
    slots, lags = lag_profile.shape
    blocks_tm, peers = lax.axis_size("tm"), lax.axis_size("clus")
    total = per_dev * peers
    half = peers // 2
    me = lax.axis_index("clus")

    def send(x, where):
        pairs = [
            (t * peers + c, u * peers + d)
            for t in range(blocks_tm)
            for c in range(peers)
            for u, d in [where(t, c)]
            if 0 <= u < blocks_tm and 0 <= d < peers
        ]
        return lax.ppermute(x, ("tm", "clus"), pairs)

    def edge(t, c):
        if c % half == half - 1:
            return t, (c + 1) % peers
        return t, ((c - 1) % peers if c % half == 0 else -1)

    wrapped = send(currents, edge)
    up = send(currents, lambda t, c: (t, c + 1 if c % half != half - 1 else -1))
    down = send(currents, lambda t, c: (t, c - 1 if c % half != 0 else -1))

    shape3 = (per_dev, steps, unknowns)
    params = lambda mib: pltpu.CompilerParams(vmem_limit_bytes=mib * MIB)
    running, totals = pl.pallas_call(
        charge_kernel,
        name="charge",
        out_shape=(
            jax.ShapeDtypeStruct(shape3, F32),
            jax.ShapeDtypeStruct((per_dev, unknowns), F32),
        ),
        in_specs=[whole()] * 2,
        out_specs=(whole(), whole()),
        compiler_params=params(32),
    )(currents, charge_map)

    def behind(x, by):
        return send(x, lambda t, c: (t + by, c))

    window = totals
    for j in (1, 2, 3):
        window = window + behind(totals, j)
    before = behind(window, 1)
    for j in (5, 9, 13):
        before = before + behind(window, j)

    first_local = (me - 1) * per_dev
    local_ids = jnp.where(neighbours >= 0, (neighbours - first_local) % total, 3 * per_dev)
    edges = jnp.stack([me % half == 0, me % half == half - 1]).astype(jnp.int32)
    lag_rows = jnp.pad(lag_profile.astype(F32), ((0, 0), (0, 2 * steps - lags)))
    lag_rows = jnp.roll(lag_rows[:, ::-1], 1, axis=1)
    head, tail = pl.pallas_call(
        near_kernel,
        name="near",
        out_shape=(
            jax.ShapeDtypeStruct(shape3, F32),
            jax.ShapeDtypeStruct(shape3, BF16),
        ),
        in_specs=[whole(pltpu.SMEM)] * 2 + [whole()] * 2 + [whole(pl.ANY)] * 4,
        out_specs=(whole(), whole()),
        scratch_shapes=[
            pltpu.VMEM((3 * per_dev + 1, steps, unknowns), BF16),
            pltpu.VMEM((slots // 2, 2 * unknowns, 2 * unknowns), BF16),
            pltpu.VMEM((2 * steps, slots * steps), BF16),
            pltpu.VMEM((4, slots * steps, 2 * unknowns), BF16),
            pltpu.SemaphoreType.DMA((3,)),
        ],
        compiler_params=params(40),
    )(local_ids, edges, lag_rows, couplings, currents, up, down, wrapped)

    tail_before = behind(tail, 1)
    base = pl.pallas_call(
        base_kernel,
        name="base",
        out_shape=jax.ShapeDtypeStruct(shape3, F32),
        in_specs=[whole()] * 5,
        out_specs=whole(),
        compiler_params=params(32),
    )(excitation, head, running, before, potential)
    return pl.pallas_call(
        final_kernel,
        name="final",
        out_shape=(
            jax.ShapeDtypeStruct(shape3, BF16),
            jax.ShapeDtypeStruct(shape3, F32),
        ),
        in_specs=[whole()] * 4,
        out_specs=(whole(), whole()),
        compiler_params=params(32),
    )(currents, base, tail_before, block_inverses)


def solution(mesh):
    in_specs = (
        P("clus", "tm", None),
        P("clus", "tm", None),
        P("clus", None),
        P(),
        P(),
        P("clus", None, None),
        P(),
        P(),
    )
    out_specs = (P("clus", "tm", None), P("clus", "tm", None))
    return jax.shard_map(
        on_device, mesh=mesh, in_specs=in_specs, out_specs=out_specs, check_vma=False
    )
```

```python
import jax
import jax.numpy as jnp
from jax import lax
from jax.experimental import pallas as pl
from jax.experimental.pallas import tpu as pltpu
from jax.sharding import PartitionSpec as P

F32, BF16 = jnp.float32, jnp.bfloat16
MIB = 1 << 20


def whole(space=pltpu.VMEM):
    return pl.BlockSpec(memory_space=space)


def dot(a, b):
    return jnp.dot(a, b, preferred_element_type=F32)


def prep_kernel(cur_ref, map_ref, coup_ref, running_ref, totals_ref):
    del coup_ref
    per_dev, steps, unknowns = cur_ref.shape
    row = lax.broadcasted_iota(jnp.int32, (steps, 2 * steps), 0)
    col = lax.broadcasted_iota(jnp.int32, (steps, 2 * steps), 1)
    lower = (row >= col % steps).astype(F32).astype(BF16)
    group = 8

    @pl.loop(0, per_dev // group)
    def _(g):
        first = g * group
        rows = cur_ref[pl.ds(first, group)].reshape(group * steps, unknowns)
        inc = dot(rows, map_ref[...])
        high = inc.astype(BF16)
        low = (inc - high.astype(F32)).astype(BF16)
        last = []
        for i in range(group):
            cut = slice(i * steps, (i + 1) * steps)
            run = dot(lower, jnp.concatenate([high[cut], low[cut]], axis=0))
            running_ref[first + i] = run
            last.append(run[steps - 1 : steps])
        totals_ref[pl.ds(first, group)] = jnp.concatenate(last, axis=0)


def near_kernel(
    ids_ref, lag_ref, own_ref, inner_ref, outer_ref, coup_ref,
    head_ref, tail_ref, field, toep_ref, terms,
):
    per_dev, steps, unknowns = own_ref.shape
    slots = coup_ref.shape[0]
    group = min(16, per_dev)
    for part, ref in enumerate((own_ref, inner_ref, outer_ref)):
        field[part * per_dev : (part + 1) * per_dev] = ref[...]
    field[3 * per_dev] = jnp.zeros((steps, unknowns), BF16)
    lane = lax.broadcasted_iota(jnp.int32, (2 * steps, 2 * steps), 1)
    for p in range(slots // 2):
        even = jnp.broadcast_to(lag_ref[2 * p : 2 * p + 1, :], lane.shape)
        odd = jnp.broadcast_to(lag_ref[2 * p + 1 : 2 * p + 2, :], lane.shape)
        even = pltpu.roll(even, 0, 1, stride=1, stride_axis=0)
        odd = pltpu.roll(odd, steps, 1, stride=1, stride_axis=0)
        both = jnp.where(lane < steps, even, odd)
        toep_ref[:, p * 2 * steps : (p + 1) * 2 * steps] = both.astype(BF16)

    @pl.loop(0, per_dev // group)
    def _(g):
        first = g * group
        for k in range(slots):
            rows = [field[ids_ref[first + i, k]] for i in range(group)]
            z = dot(jnp.concatenate(rows, axis=0), coup_ref[k]).astype(BF16)
            at = slice(k * steps, (k + 1) * steps)
            for i in range(group):
                lanes = slice((i % 2) * unknowns, (i % 2 + 1) * unknowns)
                terms[i // 2, at, lanes] = z[i * steps : (i + 1) * steps]
        for i in range(0, group, 2):
            out = dot(toep_ref[...], terms[i // 2])
            for j in range(2):
                lanes = slice(j * unknowns, (j + 1) * unknowns)
                head_ref[first + i + j] = out[:steps, lanes]
                tail_ref[first + i + j] = out[steps:, lanes].astype(BF16)


def base_kernel(exc_ref, head_ref, running_ref, sums_ref, totals_ref, pot_ref, base_ref):
    per_dev, steps, unknowns = exc_ref.shape
    group = 8

    @pl.loop(0, per_dev // group)
    def _(g):
        at = pl.ds(g * group, group)
        before = sums_ref[at] - totals_ref[at]
        charge = (running_ref[at] + before[:, None, :]).astype(BF16)
        field = dot(charge.reshape(group * steps, -1), pot_ref[...])
        field = field.reshape(group, steps, unknowns)
        base_ref[at] = exc_ref[at].astype(F32) - head_ref[at] - field


def final_kernel(cur_ref, base_ref, tail_ref, inv_ref, updated_ref, residual_ref):
    for i in range(cur_ref.shape[0]):
        residual = base_ref[i] - tail_ref[i].astype(F32)
        residual_ref[i] = residual
        correction = dot(residual.astype(BF16), inv_ref[i])
        updated_ref[i] = (cur_ref[i].astype(F32) + correction).astype(BF16)


def on_device(
    currents, excitation, neighbours, lag_profile, couplings, block_inverses, charge_map, potential
):
    per_dev, steps, unknowns = currents.shape
    slots, lags = lag_profile.shape
    blocks, peers = lax.axis_size("tm"), lax.axis_size("clus")
    me = lax.axis_index("clus")

    def send(x, where):
        pairs = [
            (t * peers + c, u * peers + d % peers)
            for t in range(blocks)
            for c in range(peers)
            for u, d in [where(t, c)]
            if 0 <= u < blocks
        ]
        return lax.ppermute(x, ("tm", "clus"), pairs)

    def behind(x, by):
        return send(x, lambda t, c: (t + by, c))

    outer = send(currents, lambda t, c: (t, c + 1 if c % 2 else c - 1))
    inner = send(currents, lambda t, c: (t, c ^ 1))

    shape3 = (per_dev, steps, unknowns)
    sds = jax.ShapeDtypeStruct
    params = lambda mib: pltpu.CompilerParams(vmem_limit_bytes=mib * MIB)
    lag_rows = jnp.pad(lag_profile.astype(F32), ((0, 0), (0, 2 * steps - lags)))
    lag_rows = jnp.roll(lag_rows[:, ::-1], 1, axis=1)
    running, totals = pl.pallas_call(
        prep_kernel,
        name="prep",
        out_shape=(
            sds(shape3, F32),
            sds((per_dev, unknowns), F32),
        ),
        in_specs=[whole()] * 3,
        out_specs=(whole(),) * 2,
        compiler_params=params(16),
    )(currents, charge_map, couplings)

    owner = neighbours // per_dev
    part = jnp.where(owner == me, 0, jnp.where(owner == me ^ 1, 1, 2))
    ids = jnp.where(neighbours >= 0, part * per_dev + neighbours % per_dev, 3 * per_dev)

    sums = totals + behind(totals, 1)
    sums = sums + behind(sums, 2)
    ids, sums = lax.optimization_barrier((ids, sums))
    head, tail = pl.pallas_call(
        near_kernel,
        name="near",
        out_shape=(sds(shape3, F32), sds(shape3, BF16)),
        in_specs=[whole(pltpu.SMEM)] + [whole()] * 5,
        out_specs=(whole(), whole()),
        scratch_shapes=[
            pltpu.VMEM((3 * per_dev + 1, steps, unknowns), BF16),
            pltpu.VMEM((2 * steps, slots * steps), BF16),
            pltpu.VMEM((8, slots * steps, 2 * unknowns), BF16),
        ],
        compiler_params=params(24),
        cost_estimate=pl.CostEstimate(
            flops=2 * per_dev * slots * steps * unknowns * (unknowns + 2 * steps),
            bytes_accessed=8 * MIB,
            transcendentals=0,
        ),
    )(ids, lag_rows, currents, inner, outer, couplings)

    tail_before = behind(tail, 1)
    sums, head = lax.optimization_barrier((sums, head))
    by = 4
    while by < blocks:
        sums = sums + behind(sums, by)
        by *= 2
    base = pl.pallas_call(
        base_kernel,
        name="base",
        out_shape=sds(shape3, F32),
        in_specs=[whole()] * 6,
        out_specs=whole(),
        compiler_params=params(16),
    )(excitation, head, running, sums, totals, potential)
    return pl.pallas_call(
        final_kernel,
        name="final",
        out_shape=(sds(shape3, BF16), sds(shape3, F32)),
        in_specs=[whole()] * 4,
        out_specs=(whole(), whole()),
        compiler_params=params(16),
    )(currents, base, tail_before, block_inverses)


def solution(mesh):
    in_specs = (
        P("clus", "tm", None),
        P("clus", "tm", None),
        P("clus", None),
        P(),
        P(),
        P("clus", None, None),
        P(),
        P(),
    )
    out_specs = (P("clus", "tm", None), P("clus", "tm", None))
    return jax.shard_map(
        on_device, mesh=mesh, in_specs=in_specs, out_specs=out_specs, check_vma=False
    )
```

```python
import jax
import jax.numpy as jnp
from jax import lax
from jax.experimental import pallas as pl
from jax.experimental.pallas import tpu as pltpu
from jax.sharding import PartitionSpec as P

F32, BF16 = jnp.float32, jnp.bfloat16
MIB = 1 << 20


def whole(space=pltpu.VMEM):
    return pl.BlockSpec(memory_space=space)


def dot(a, b):
    return jnp.dot(a, b, preferred_element_type=F32)


def prep_kernel(cur_ref, map_ref, running_ref, totals_ref):
    per_dev, steps, unknowns = cur_ref.shape
    row = lax.broadcasted_iota(jnp.int32, (steps, 2 * steps), 0)
    col = lax.broadcasted_iota(jnp.int32, (steps, 2 * steps), 1)
    lower = (row >= col % steps).astype(F32).astype(BF16)
    group = 8

    @pl.loop(0, per_dev // group)
    def _(g):
        first = g * group
        rows = cur_ref[pl.ds(first, group)].reshape(group * steps, unknowns)
        inc = dot(rows, map_ref[...])
        high = inc.astype(BF16)
        low = (inc - high.astype(F32)).astype(BF16)
        last = []
        for i in range(group):
            cut = slice(i * steps, (i + 1) * steps)
            run = dot(lower, jnp.concatenate([high[cut], low[cut]], axis=0))
            running_ref[first + i] = run
            last.append(run[steps - 1 : steps])
        totals_ref[pl.ds(first, group)] = jnp.concatenate(last, axis=0)


def near_kernel(
    ids_ref, lag_ref, own_ref, inner_ref, outer_ref, coup_hbm,
    head_ref, tail_ref, field, coup_ref, toep_ref, terms, sems,
):
    per_dev, steps, unknowns = own_ref.shape
    slots = coup_ref.shape[0]
    group = min(16, per_dev)
    copies = [pltpu.make_async_copy(coup_hbm, coup_ref, sems.at[3])]
    for part, ref in enumerate((own_ref, inner_ref, outer_ref)):
        to = field.at[pl.ds(part * per_dev, per_dev)]
        copies.append(pltpu.make_async_copy(ref, to, sems.at[part]))
    for copy in copies:
        copy.start()
    field[3 * per_dev] = jnp.zeros((steps, unknowns), BF16)
    lane = lax.broadcasted_iota(jnp.int32, (2 * steps, 2 * steps), 1)
    for p in range(slots // 2):
        even = jnp.broadcast_to(lag_ref[2 * p : 2 * p + 1, :], lane.shape)
        odd = jnp.broadcast_to(lag_ref[2 * p + 1 : 2 * p + 2, :], lane.shape)
        even = pltpu.roll(even, 0, 1, stride=1, stride_axis=0)
        odd = pltpu.roll(odd, steps, 1, stride=1, stride_axis=0)
        both = jnp.where(lane < steps, even, odd)
        toep_ref[:, p * 2 * steps : (p + 1) * 2 * steps] = both.astype(BF16)
    for copy in copies:
        copy.wait()

    @pl.loop(0, per_dev // group)
    def _(g):
        first = g * group
        for k in range(slots):
            rows = [field[ids_ref[first + i, k]] for i in range(group)]
            z = dot(jnp.concatenate(rows, axis=0), coup_ref[k]).astype(BF16)
            at = slice(k * steps, (k + 1) * steps)
            for i in range(group):
                lanes = slice((i % 2) * unknowns, (i % 2 + 1) * unknowns)
                terms[i // 2, at, lanes] = z[i * steps : (i + 1) * steps]
        for i in range(0, group, 2):
            out = dot(toep_ref[...], terms[i // 2])
            for j in range(2):
                lanes = slice(j * unknowns, (j + 1) * unknowns)
                head_ref[first + i + j] = out[:steps, lanes]
                tail_ref[first + i + j] = out[steps:, lanes].astype(BF16)


def base_kernel(exc_ref, head_ref, running_ref, before_ref, pot_ref, base_ref):
    per_dev, steps, unknowns = exc_ref.shape
    group = 8

    @pl.loop(0, per_dev // group)
    def _(g):
        at = pl.ds(g * group, group)
        charge = (running_ref[at] + before_ref[at][:, None, :]).astype(BF16)
        field = dot(charge.reshape(group * steps, -1), pot_ref[...])
        field = field.reshape(group, steps, unknowns)
        base_ref[at] = exc_ref[at].astype(F32) - head_ref[at] - field


def final_kernel(cur_ref, base_ref, tail_ref, inv_ref, updated_ref, residual_ref):
    for i in range(cur_ref.shape[0]):
        residual = base_ref[i] - tail_ref[i].astype(F32)
        residual_ref[i] = residual
        correction = dot(residual.astype(BF16), inv_ref[i])
        updated_ref[i] = (cur_ref[i].astype(F32) + correction).astype(BF16)


def on_device(
    currents, excitation, neighbours, lag_profile, couplings, block_inverses, charge_map, potential
):
    per_dev, steps, unknowns = currents.shape
    slots, lags = lag_profile.shape
    blocks, peers = lax.axis_size("tm"), lax.axis_size("clus")
    me = lax.axis_index("clus")

    def send(x, where):
        pairs = [
            (t * peers + c, u * peers + d % peers)
            for t in range(blocks)
            for c in range(peers)
            for u, d in [where(t, c)]
            if 0 <= u < blocks
        ]
        return lax.ppermute(x, ("tm", "clus"), pairs)

    def behind(x, by):
        return send(x, lambda t, c: (t + by, c))

    outer = send(currents, lambda t, c: (t, c + 1 if c % 2 else c - 1))
    inner = send(currents, lambda t, c: (t, c ^ 1))

    shape3 = (per_dev, steps, unknowns)
    sds = jax.ShapeDtypeStruct
    params = lambda mib: pltpu.CompilerParams(vmem_limit_bytes=mib * MIB)
    lag_rows = jnp.pad(lag_profile.astype(F32), ((0, 0), (0, 2 * steps - lags)))
    lag_rows = jnp.roll(lag_rows[:, ::-1], 1, axis=1)
    running, totals = pl.pallas_call(
        prep_kernel,
        name="prep",
        out_shape=(
            sds(shape3, F32),
            sds((per_dev, unknowns), F32),
        ),
        in_specs=[whole()] * 2,
        out_specs=(whole(),) * 2,
        compiler_params=params(16),
    )(currents, charge_map)

    owner = neighbours // per_dev
    part = jnp.where(owner == me, 0, jnp.where(owner == me ^ 1, 1, 2))
    ids = jnp.where(neighbours >= 0, part * per_dev + neighbours % per_dev, 3 * per_dev)

    later = jnp.arange(blocks) > lax.axis_index("tm")
    before = lax.psum_scatter(
        jnp.where(later[:, None, None], totals, 0.0), "tm", scatter_dimension=0
    )
    ids, running = lax.optimization_barrier((ids, running))
    head, tail = pl.pallas_call(
        near_kernel,
        name="near",
        out_shape=(sds(shape3, F32), sds(shape3, BF16)),
        in_specs=[whole(pltpu.SMEM), whole()] + [whole(pl.ANY)] * 4,
        out_specs=(whole(), whole()),
        scratch_shapes=[
            pltpu.VMEM((3 * per_dev + 1, steps, unknowns), BF16),
            pltpu.VMEM(couplings.shape, BF16),
            pltpu.VMEM((2 * steps, slots * steps), BF16),
            pltpu.VMEM((8, slots * steps, 2 * unknowns), BF16),
            pltpu.SemaphoreType.DMA((4,)),
        ],
        compiler_params=params(56),
        cost_estimate=pl.CostEstimate(
            flops=2 * per_dev * slots * steps * unknowns * (unknowns + 2 * steps),
            bytes_accessed=8 * MIB,
            transcendentals=0,
        ),
    )(ids, lag_rows, currents, inner, outer, couplings)

    tail_before = behind(tail, 1)
    base = pl.pallas_call(
        base_kernel,
        name="base",
        out_shape=sds(shape3, F32),
        in_specs=[whole()] * 5,
        out_specs=whole(),
        compiler_params=params(16),
    )(excitation, head, running, before, potential)
    return pl.pallas_call(
        final_kernel,
        name="final",
        out_shape=(sds(shape3, BF16), sds(shape3, F32)),
        in_specs=[whole()] * 4,
        out_specs=(whole(), whole()),
        compiler_params=params(16),
    )(currents, base, tail_before, block_inverses)


def solution(mesh):
    in_specs = (
        P("clus", "tm", None),
        P("clus", "tm", None),
        P("clus", None),
        P(),
        P(),
        P("clus", None, None),
        P(),
        P(),
    )
    out_specs = (P("clus", "tm", None), P("clus", "tm", None))
    return jax.shard_map(
        on_device, mesh=mesh, in_specs=in_specs, out_specs=out_specs, check_vma=False
    )
```

```python
import jax
import jax.numpy as jnp
from jax import lax
from jax.experimental import pallas as pl
from jax.experimental.pallas import tpu as pltpu
from jax.sharding import PartitionSpec as P

F32, BF16 = jnp.float32, jnp.bfloat16
MIB = 1 << 20


def whole(space=pltpu.VMEM):
    return pl.BlockSpec(memory_space=space)


def dot(a, b):
    return jnp.dot(a, b, preferred_element_type=F32)


def prep_kernel(cur_ref, map_ref, running_ref, totals_ref):
    per_dev, steps, unknowns = cur_ref.shape
    row = lax.broadcasted_iota(jnp.int32, (steps, 2 * steps), 0)
    col = lax.broadcasted_iota(jnp.int32, (steps, 2 * steps), 1)
    lower = (row >= col % steps).astype(F32).astype(BF16)
    group = 8

    @pl.loop(0, per_dev // group)
    def _(g):
        first = g * group
        rows = cur_ref[pl.ds(first, group)].reshape(group * steps, unknowns)
        inc = dot(rows, map_ref[...])
        high = inc.astype(BF16)
        low = (inc - high.astype(F32)).astype(BF16)
        last = []
        for i in range(group):
            cut = slice(i * steps, (i + 1) * steps)
            run = dot(lower, jnp.concatenate([high[cut], low[cut]], axis=0))
            running_ref[first + i] = run
            last.append(run[steps - 1 : steps])
        totals = jnp.concatenate(last, axis=0)
        for t in range(totals_ref.shape[0]):
            totals_ref[t, pl.ds(first, group)] = totals


def factor_kernel(lag_ref, coup_ref, own_ref, inner_ref, toep_ref, copy_ref, known_ref):
    slots = lag_ref.shape[0]
    steps = toep_ref.shape[1] // slots
    lane = lax.broadcasted_iota(jnp.int32, (2 * steps, 2 * steps), 1)
    for p in range(slots // 2):
        even = jnp.broadcast_to(lag_ref[2 * p : 2 * p + 1, :], lane.shape)
        odd = jnp.broadcast_to(lag_ref[2 * p + 1 : 2 * p + 2, :], lane.shape)
        even = pltpu.roll(even, 0, 1, stride=1, stride_axis=0)
        odd = pltpu.roll(odd, steps, 1, stride=1, stride_axis=0)
        both = jnp.where(lane < steps, even, odd)
        toep_ref[:, p * 2 * steps : (p + 1) * 2 * steps] = both.astype(BF16)
    copy_ref[...] = coup_ref[...]
    per_dev = own_ref.shape[0]
    known_ref[:per_dev] = own_ref[...]
    known_ref[per_dev:] = inner_ref[...]


def near_kernel(
    ids_ref, known_ref, outer_ref, coup_ref, toep_ref,
    head_ref, tail_ref, field, terms,
):
    per_dev, steps, unknowns = outer_ref.shape
    slots = coup_ref.shape[0]
    group = min(16, per_dev)
    field[: 2 * per_dev] = known_ref[...]
    field[2 * per_dev : 3 * per_dev] = outer_ref[...]
    field[3 * per_dev] = jnp.zeros((steps, unknowns), BF16)

    @pl.loop(0, per_dev // group)
    def _(g):
        first = g * group
        for k in range(slots):
            rows = [field[ids_ref[first + i, k]] for i in range(group)]
            z = dot(jnp.concatenate(rows, axis=0), coup_ref[k]).astype(BF16)
            at = slice(k * steps, (k + 1) * steps)
            for i in range(group):
                lanes = slice((i % 2) * unknowns, (i % 2 + 1) * unknowns)
                terms[i // 2, at, lanes] = z[i * steps : (i + 1) * steps]
        for i in range(0, group, 2):
            out = dot(toep_ref[...], terms[i // 2])
            for j in range(2):
                lanes = slice(j * unknowns, (j + 1) * unknowns)
                head_ref[first + i + j] = out[:steps, lanes]
                tail_ref[first + i + j] = out[steps:, lanes].astype(BF16)


def base_kernel(exc_ref, head_ref, running_ref, before_ref, pot_ref, base_ref):
    per_dev, steps, unknowns = exc_ref.shape
    group = 8

    @pl.loop(0, per_dev // group)
    def _(g):
        at = pl.ds(g * group, group)
        charge = (running_ref[at] + before_ref[at][:, None, :]).astype(BF16)
        field = dot(charge.reshape(group * steps, -1), pot_ref[...])
        field = field.reshape(group, steps, unknowns)
        base_ref[at] = exc_ref[at].astype(F32) - head_ref[at] - field


def final_kernel(cur_ref, base_ref, tail_ref, inv_ref, updated_ref, residual_ref):
    for i in range(cur_ref.shape[0]):
        residual = base_ref[i] - tail_ref[i].astype(F32)
        residual_ref[i] = residual
        correction = dot(residual.astype(BF16), inv_ref[i])
        updated_ref[i] = (cur_ref[i].astype(F32) + correction).astype(BF16)


def on_device(
    currents, excitation, neighbours, lag_profile, couplings, block_inverses, charge_map, potential
):
    per_dev, steps, unknowns = currents.shape
    slots, lags = lag_profile.shape
    blocks, peers = lax.axis_size("tm"), lax.axis_size("clus")
    me = lax.axis_index("clus")

    def send(x, where):
        pairs = [
            (t * peers + c, u * peers + d % peers)
            for t in range(blocks)
            for c in range(peers)
            for u, d in [where(t, c)]
            if 0 <= u < blocks
        ]
        return lax.ppermute(x, ("tm", "clus"), pairs)

    def behind(x, by):
        return send(x, lambda t, c: (t + by, c))

    outer = send(currents, lambda t, c: (t, c + 1 if c % 2 else c - 1))
    inner = send(currents, lambda t, c: (t, c ^ 1))

    shape3 = (per_dev, steps, unknowns)
    sds = jax.ShapeDtypeStruct
    params = lambda mib: pltpu.CompilerParams(vmem_limit_bytes=mib * MIB)
    lag_rows = jnp.pad(lag_profile.astype(F32), ((0, 0), (0, 2 * steps - lags)))
    lag_rows = jnp.roll(lag_rows[:, ::-1], 1, axis=1)
    running, totals = pl.pallas_call(
        prep_kernel,
        name="prep",
        out_shape=(
            sds(shape3, F32),
            sds((blocks, per_dev, unknowns), F32),
        ),
        in_specs=[whole()] * 2,
        out_specs=(whole(),) * 2,
        compiler_params=params(16),
    )(currents, charge_map)

    owner = neighbours // per_dev
    part = jnp.where(owner == me, 0, jnp.where(owner == me ^ 1, 1, 2))
    ids = jnp.where(neighbours >= 0, part * per_dev + neighbours % per_dev, 3 * per_dev)

    pieces = lax.all_to_all(totals, "tm", 0, 0)
    lag_rows, couplings, running = lax.optimization_barrier((lag_rows, couplings, running))
    toeplitz, factors, known = pl.pallas_call(
        factor_kernel,
        name="factors",
        out_shape=(
            sds((2 * steps, slots * steps), BF16),
            sds(couplings.shape, BF16),
            sds((2 * per_dev, steps, unknowns), BF16),
        ),
        in_specs=[whole()] * 4,
        out_specs=(whole(),) * 3,
        compiler_params=params(16),
    )(lag_rows, couplings, currents, inner)
    head, tail = pl.pallas_call(
        near_kernel,
        name="near",
        out_shape=(sds(shape3, F32), sds(shape3, BF16)),
        in_specs=[whole(pltpu.SMEM)] + [whole()] * 4,
        out_specs=(whole(), whole()),
        scratch_shapes=[
            pltpu.VMEM((3 * per_dev + 1, steps, unknowns), BF16),
            pltpu.VMEM((8, slots * steps, 2 * unknowns), BF16),
        ],
        compiler_params=params(24),
        cost_estimate=pl.CostEstimate(
            flops=2 * per_dev * slots * steps * unknowns * (unknowns + 2 * steps),
            bytes_accessed=8 * MIB,
            transcendentals=0,
        ),
    )(ids, known, outer, factors, toeplitz)

    tail_before = behind(tail, 1)
    earlier = jnp.arange(blocks) < lax.axis_index("tm")
    pieces, head = lax.optimization_barrier((pieces, head))
    before = jnp.sum(jnp.where(earlier[:, None, None], pieces, 0.0), axis=0)
    base = pl.pallas_call(
        base_kernel,
        name="base",
        out_shape=sds(shape3, F32),
        in_specs=[whole()] * 5,
        out_specs=whole(),
        compiler_params=params(16),
    )(excitation, head, running, before, potential)
    return pl.pallas_call(
        final_kernel,
        name="final",
        out_shape=(sds(shape3, BF16), sds(shape3, F32)),
        in_specs=[whole()] * 4,
        out_specs=(whole(), whole()),
        compiler_params=params(16),
    )(currents, base, tail_before, block_inverses)


def solution(mesh):
    in_specs = (
        P("clus", "tm", None),
        P("clus", "tm", None),
        P("clus", None),
        P(),
        P(),
        P("clus", None, None),
        P(),
        P(),
    )
    out_specs = (P("clus", "tm", None), P("clus", "tm", None))
    return jax.shard_map(
        on_device, mesh=mesh, in_specs=in_specs, out_specs=out_specs, check_vma=False
    )
```

```python
import jax
import jax.numpy as jnp
from jax import lax
from jax.experimental import pallas as pl
from jax.experimental.pallas import tpu as pltpu
from jax.sharding import PartitionSpec as P

F32, BF16 = jnp.float32, jnp.bfloat16
MIB = 1 << 20
LANE = 4


def whole(space=pltpu.VMEM):
    return pl.BlockSpec(memory_space=space)


def dot(a, b):
    return jnp.dot(a, b, preferred_element_type=F32)


def prep_kernel(cur_ref, map_ref, running_ref, totals_ref):
    per_dev, steps, unknowns = cur_ref.shape
    row = lax.broadcasted_iota(jnp.int32, (steps, 2 * steps), 0)
    col = lax.broadcasted_iota(jnp.int32, (steps, 2 * steps), 1)
    lower = (row >= col % steps).astype(F32).astype(BF16)
    group = 8

    @pl.loop(0, per_dev // group)
    def _(g):
        first = g * group
        rows = cur_ref[pl.ds(first, group)].reshape(group * steps, unknowns)
        inc = dot(rows, map_ref[...])
        high = inc.astype(BF16)
        low = (inc - high.astype(F32)).astype(BF16)
        last = []
        for i in range(group):
            cut = slice(i * steps, (i + 1) * steps)
            run = dot(lower, jnp.concatenate([high[cut], low[cut]], axis=0))
            running_ref[first + i] = run
            last.append(run[steps - 1 : steps])
        totals = jnp.concatenate(last, axis=0)
        for t in range(totals_ref.shape[0]):
            totals_ref[t, pl.ds(first, group)] = totals


def layout_kernel(
    edge_ref, lag_ref, own_ref, inner_ref, outer_ref, nearer_ref, relayed_ref, field_ref, toep_ref,
):
    per_dev, steps, unknowns = own_ref.shape
    slots = lag_ref.shape[0]
    lane = lax.broadcasted_iota(jnp.int32, (2 * steps, 2 * steps), 1)
    for p in range(slots // 2):
        even = jnp.broadcast_to(lag_ref[2 * p : 2 * p + 1, :], lane.shape)
        odd = jnp.broadcast_to(lag_ref[2 * p + 1 : 2 * p + 2, :], lane.shape)
        even = pltpu.roll(even, 0, 1, stride=1, stride_axis=0)
        odd = pltpu.roll(odd, steps, 1, stride=1, stride_axis=0)
        both = jnp.where(lane < steps, even, odd)
        toep_ref[:, p * 2 * steps : (p + 1) * 2 * steps] = both.astype(BF16)
    cut = 2 * per_dev + outer_ref.shape[0]
    field_ref[:per_dev] = own_ref[...]
    field_ref[per_dev : 2 * per_dev] = inner_ref[...]
    field_ref[2 * per_dev : cut] = outer_ref[...]
    field_ref[3 * per_dev] = jnp.zeros((steps, unknowns), BF16)

    @pl.when(edge_ref[0] > 0)
    def _():
        field_ref[cut : 3 * per_dev] = relayed_ref[...]

    @pl.when(edge_ref[0] <= 0)
    def _():
        field_ref[cut : 3 * per_dev] = nearer_ref[...]


def near_kernel(
    ids_ref, field, coup_ref, toep_ref, head_ref, tail_ref, terms,
):
    per_dev, steps, unknowns = head_ref.shape
    slots = coup_ref.shape[0]
    group = min(16, per_dev)

    @pl.loop(0, per_dev // group)
    def _(g):
        first = g * group
        for k in range(slots):
            rows = [field[ids_ref[first + i, k]] for i in range(group)]
            z = dot(jnp.concatenate(rows, axis=0), coup_ref[k]).astype(BF16)
            at = slice(k * steps, (k + 1) * steps)
            for i in range(group):
                lanes = slice((i % 2) * unknowns, (i % 2 + 1) * unknowns)
                terms[i // 2, at, lanes] = z[i * steps : (i + 1) * steps]
        for i in range(0, group, 2):
            out = dot(toep_ref[...], terms[i // 2])
            for j in range(2):
                lanes = slice(j * unknowns, (j + 1) * unknowns)
                head_ref[first + i + j] = out[:steps, lanes]
                tail_ref[first + i + j] = out[steps:, lanes].astype(BF16)


def base_kernel(exc_ref, head_ref, running_ref, before_ref, pot_ref, base_ref):
    per_dev, steps, unknowns = exc_ref.shape
    group = 8

    @pl.loop(0, per_dev // group)
    def _(g):
        at = pl.ds(g * group, group)
        charge = (running_ref[at] + before_ref[at][:, None, :]).astype(BF16)
        field = dot(charge.reshape(group * steps, -1), pot_ref[...])
        field = field.reshape(group, steps, unknowns)
        base_ref[at] = exc_ref[at].astype(F32) - head_ref[at] - field


def final_kernel(cur_ref, base_ref, tail_ref, inv_ref, updated_ref, residual_ref):
    for i in range(cur_ref.shape[0]):
        residual = base_ref[i] - tail_ref[i].astype(F32)
        residual_ref[i] = residual
        correction = dot(residual.astype(BF16), inv_ref[i])
        updated_ref[i] = (cur_ref[i].astype(F32) + correction).astype(BF16)


def on_device(
    currents, excitation, neighbours, lag_profile, couplings, block_inverses, charge_map, potential
):
    per_dev, steps, unknowns = currents.shape
    slots, lags = lag_profile.shape
    blocks, peers = lax.axis_size("tm"), lax.axis_size("clus")
    me = lax.axis_index("clus")

    def send(x, where):
        pairs = [
            (t * peers + c, u * peers + d % peers)
            for t in range(blocks)
            for c in range(peers)
            for u, d in [where(t, c)]
            if 0 <= u < blocks
        ]
        return lax.ppermute(x, ("tm", "clus"), pairs)

    def behind(x, by):
        return send(x, lambda t, c: (t + by, c))

    lane, half = min(LANE, blocks), peers // 2

    def is_wrap(c):
        return c % half in (0, half - 1)

    def along(t, c, by):
        z = (c // half * lane + t % lane + by) % (2 * lane)
        return t // lane * lane + z % lane, z // lane * half + c % half

    def across(t, c):
        return t, c + 1 if c % 2 else c - 1

    def opposite(t, c):
        return t, c // half * half + half - 1 - c % half

    kept = 5 * per_dev // 8
    outer = send(currents[:kept], across)
    nearer = send(
        currents[kept:], lambda t, c: along(t, c, 1) if is_wrap(c) else across(t, c)
    )

    inner = send(currents, lambda t, c: (t, c ^ 1))
    relayed = send(
        nearer,
        lambda t, c: opposite(*along(t, c, lane - 1)) if is_wrap(c) else (blocks, c),
    )
    is_edge = ((me % half == 0) | (me % half == half - 1)).astype(jnp.int32).reshape(1)

    shape3 = (per_dev, steps, unknowns)
    sds = jax.ShapeDtypeStruct
    params = lambda mib: pltpu.CompilerParams(vmem_limit_bytes=mib * MIB)
    lag_rows = jnp.pad(lag_profile.astype(F32), ((0, 0), (0, 2 * steps - lags)))
    lag_rows = jnp.roll(lag_rows[:, ::-1], 1, axis=1)
    running, totals = pl.pallas_call(
        prep_kernel,
        name="prep",
        out_shape=(
            sds(shape3, F32),
            sds((blocks, per_dev, unknowns), F32),
        ),
        in_specs=[whole()] * 2,
        out_specs=(whole(),) * 2,
        compiler_params=params(16),
    )(currents, charge_map)

    owner = neighbours // per_dev
    part = jnp.where(owner == me, 0, jnp.where(owner == me ^ 1, 1, 2))
    ids = jnp.where(neighbours >= 0, part * per_dev + neighbours % per_dev, 3 * per_dev)

    lag_rows, running = lax.optimization_barrier((lag_rows, running))
    totals, nearer = lax.optimization_barrier((totals, nearer))
    pieces = lax.all_to_all(totals, "tm", 0, 0)
    field, toeplitz = pl.pallas_call(
        layout_kernel,
        name="layout",
        out_shape=(
            sds((3 * per_dev + 1, steps, unknowns), BF16),
            sds((2 * steps, slots * steps), BF16),
        ),
        in_specs=[whole(pltpu.SMEM)] + [whole()] * 6,
        out_specs=(whole(), whole()),
        compiler_params=params(16),
    )(is_edge, lag_rows, currents, inner, outer, nearer, relayed)
    head, tail = pl.pallas_call(
        near_kernel,
        name="near",
        out_shape=(sds(shape3, F32), sds(shape3, BF16)),
        in_specs=[whole(pltpu.SMEM)] + [whole()] * 3,
        out_specs=(whole(), whole()),
        scratch_shapes=[
            pltpu.VMEM((8, slots * steps, 2 * unknowns), BF16),
        ],
        compiler_params=params(24),
        cost_estimate=pl.CostEstimate(
            flops=2 * per_dev * slots * steps * unknowns * (unknowns + 2 * steps),
            bytes_accessed=8 * MIB,
            transcendentals=0,
        ),
    )(ids, field, couplings, toeplitz)

    tail_before = behind(tail, 1)
    earlier = jnp.arange(blocks) < lax.axis_index("tm")
    pieces, head = lax.optimization_barrier((pieces, head))
    before = jnp.sum(jnp.where(earlier[:, None, None], pieces, 0.0), axis=0)
    base = pl.pallas_call(
        base_kernel,
        name="base",
        out_shape=sds(shape3, F32),
        in_specs=[whole()] * 5,
        out_specs=whole(),
        compiler_params=params(16),
    )(excitation, head, running, before, potential)
    return pl.pallas_call(
        final_kernel,
        name="final",
        out_shape=(sds(shape3, BF16), sds(shape3, F32)),
        in_specs=[whole()] * 4,
        out_specs=(whole(), whole()),
        compiler_params=params(16),
    )(currents, base, tail_before, block_inverses)


def solution(mesh):
    in_specs = (
        P("clus", "tm", None),
        P("clus", "tm", None),
        P("clus", None),
        P(),
        P(),
        P("clus", None, None),
        P(),
        P(),
    )
    out_specs = (P("clus", "tm", None), P("clus", "tm", None))
    return jax.shard_map(
        on_device, mesh=mesh, in_specs=in_specs, out_specs=out_specs, check_vma=False
    )
```

```python
import jax
import jax.numpy as jnp
from jax import lax
from jax.experimental import pallas as pl
from jax.experimental.pallas import tpu as pltpu
from jax.sharding import PartitionSpec as P

F32, BF16 = jnp.float32, jnp.bfloat16
MIB = 1 << 20


def whole(space=pltpu.VMEM):
    return pl.BlockSpec(memory_space=space)


def dot(a, b):
    return jnp.dot(a, b, preferred_element_type=F32)


def prep_kernel(cur_ref, map_ref, running_ref, totals_ref):
    per_dev, steps, unknowns = cur_ref.shape
    row = lax.broadcasted_iota(jnp.int32, (steps, 2 * steps), 0)
    col = lax.broadcasted_iota(jnp.int32, (steps, 2 * steps), 1)
    lower = (row >= col % steps).astype(F32).astype(BF16)
    group = 8

    @pl.loop(0, per_dev // group)
    def _(g):
        first = g * group
        rows = cur_ref[pl.ds(first, group)].reshape(group * steps, unknowns)
        inc = dot(rows, map_ref[...])
        high = inc.astype(BF16)
        low = (inc - high.astype(F32)).astype(BF16)
        last = []
        for i in range(group):
            cut = slice(i * steps, (i + 1) * steps)
            run = dot(lower, jnp.concatenate([high[cut], low[cut]], axis=0))
            running_ref[first + i] = run
            last.append(run[steps - 1 : steps])
        totals = jnp.concatenate(last, axis=0)
        for t in range(totals_ref.shape[0]):
            totals_ref[t, pl.ds(first, group)] = totals


def layout_kernel(lag_ref, own_ref, inner_ref, outer_ref, field_ref, toep_ref):
    per_dev, steps, unknowns = own_ref.shape
    slots = lag_ref.shape[0]
    lane = lax.broadcasted_iota(jnp.int32, (2 * steps, 2 * steps), 1)
    for p in range(slots // 2):
        even = jnp.broadcast_to(lag_ref[2 * p : 2 * p + 1, :], lane.shape)
        odd = jnp.broadcast_to(lag_ref[2 * p + 1 : 2 * p + 2, :], lane.shape)
        even = pltpu.roll(even, 0, 1, stride=1, stride_axis=0)
        odd = pltpu.roll(odd, steps, 1, stride=1, stride_axis=0)
        both = jnp.where(lane < steps, even, odd)
        toep_ref[:, p * 2 * steps : (p + 1) * 2 * steps] = both.astype(BF16)
    for part, ref in enumerate((own_ref, inner_ref, outer_ref)):
        field_ref[part * per_dev : (part + 1) * per_dev] = ref[...]
    field_ref[3 * per_dev] = jnp.zeros((steps, unknowns), BF16)


def near_kernel(
    ids_ref, field, coup_ref, toep_ref, head_ref, tail_ref, terms,
):
    per_dev, steps, unknowns = head_ref.shape
    slots = coup_ref.shape[0]
    group = min(16, per_dev)

    @pl.loop(0, per_dev // group)
    def _(g):
        first = g * group
        for k in range(slots):
            rows = [field[ids_ref[first + i, k]] for i in range(group)]
            z = dot(jnp.concatenate(rows, axis=0), coup_ref[k]).astype(BF16)
            at = slice(k * steps, (k + 1) * steps)
            for i in range(group):
                lanes = slice((i % 2) * unknowns, (i % 2 + 1) * unknowns)
                terms[i // 2, at, lanes] = z[i * steps : (i + 1) * steps]
        for i in range(0, group, 2):
            out = dot(toep_ref[...], terms[i // 2])
            for j in range(2):
                lanes = slice(j * unknowns, (j + 1) * unknowns)
                head_ref[first + i + j] = out[:steps, lanes]
                tail_ref[first + i + j] = out[steps:, lanes].astype(BF16)


def base_kernel(exc_ref, head_ref, running_ref, before_ref, pot_ref, base_ref):
    per_dev, steps, unknowns = exc_ref.shape
    group = 8

    @pl.loop(0, per_dev // group)
    def _(g):
        at = pl.ds(g * group, group)
        charge = (running_ref[at] + before_ref[at][:, None, :]).astype(BF16)
        field = dot(charge.reshape(group * steps, -1), pot_ref[...])
        field = field.reshape(group, steps, unknowns)
        base_ref[at] = exc_ref[at].astype(F32) - head_ref[at] - field


def final_kernel(cur_ref, base_ref, tail_ref, inv_ref, updated_ref, residual_ref):
    for i in range(cur_ref.shape[0]):
        residual = base_ref[i] - tail_ref[i].astype(F32)
        residual_ref[i] = residual
        correction = dot(residual.astype(BF16), inv_ref[i])
        updated_ref[i] = (cur_ref[i].astype(F32) + correction).astype(BF16)


def on_device(
    currents, excitation, neighbours, lag_profile, couplings, block_inverses, charge_map, potential
):
    per_dev, steps, unknowns = currents.shape
    slots, lags = lag_profile.shape
    blocks, peers = lax.axis_size("tm"), lax.axis_size("clus")
    me = lax.axis_index("clus")

    def send(x, where):
        pairs = [
            (t * peers + c, u * peers + d % peers)
            for t in range(blocks)
            for c in range(peers)
            for u, d in [where(t, c)]
            if 0 <= u < blocks
        ]
        return lax.ppermute(x, ("tm", "clus"), pairs)

    def behind(x, by):
        return send(x, lambda t, c: (t + by, c))

    outer = send(currents, lambda t, c: (t, c + 1 if c % 2 else c - 1))
    inner = send(currents, lambda t, c: (t, c ^ 1))
    shape3 = (per_dev, steps, unknowns)
    sds = jax.ShapeDtypeStruct
    params = lambda mib: pltpu.CompilerParams(vmem_limit_bytes=mib * MIB)
    lag_rows = jnp.pad(lag_profile.astype(F32), ((0, 0), (0, 2 * steps - lags)))
    lag_rows = jnp.roll(lag_rows[:, ::-1], 1, axis=1)
    running, totals = pl.pallas_call(
        prep_kernel,
        name="prep",
        out_shape=(
            sds(shape3, F32),
            sds((blocks, per_dev, unknowns), F32),
        ),
        in_specs=[whole()] * 2,
        out_specs=(whole(),) * 2,
        compiler_params=params(16),
    )(currents, charge_map)

    owner = neighbours // per_dev
    part = jnp.where(owner == me, 0, jnp.where(owner == me ^ 1, 1, 2))
    ids = jnp.where(neighbours >= 0, part * per_dev + neighbours % per_dev, 3 * per_dev)

    lag_rows, running = lax.optimization_barrier((lag_rows, running))
    pieces = lax.all_to_all(totals, "tm", 0, 0)
    field, toeplitz = pl.pallas_call(
        layout_kernel,
        name="layout",
        out_shape=(
            sds((3 * per_dev + 1, steps, unknowns), BF16),
            sds((2 * steps, slots * steps), BF16),
        ),
        in_specs=[whole()] * 4,
        out_specs=(whole(), whole()),
        compiler_params=params(16),
    )(lag_rows, currents, inner, outer)
    head, tail = pl.pallas_call(
        near_kernel,
        name="near",
        out_shape=(sds(shape3, F32), sds(shape3, BF16)),
        in_specs=[whole(pltpu.SMEM)] + [whole()] * 3,
        out_specs=(whole(), whole()),
        scratch_shapes=[
            pltpu.VMEM((8, slots * steps, 2 * unknowns), BF16),
        ],
        compiler_params=params(24),
        cost_estimate=pl.CostEstimate(
            flops=2 * per_dev * slots * steps * unknowns * (unknowns + 2 * steps),
            bytes_accessed=8 * MIB,
            transcendentals=0,
        ),
    )(ids, field, couplings, toeplitz)

    tail_before = behind(tail, 1)
    earlier = jnp.arange(blocks) < lax.axis_index("tm")
    pieces, head = lax.optimization_barrier((pieces, head))
    before = jnp.sum(jnp.where(earlier[:, None, None], pieces, 0.0), axis=0)
    def piece(rows):
        return pl.BlockSpec((per_dev // 4, rows, unknowns), lambda i: (i, 0, 0))

    base = pl.pallas_call(
        base_kernel,
        name="base",
        out_shape=sds(shape3, F32),
        in_specs=[whole()] * 5,
        out_specs=whole(),
        compiler_params=params(16),
    )(excitation, head, running, before, potential)
    return pl.pallas_call(
        final_kernel,
        name="final",
        out_shape=(sds(shape3, BF16), sds(shape3, F32)),
        grid=(4,),
        in_specs=[piece(steps)] * 3 + [piece(unknowns)],
        out_specs=(piece(steps), piece(steps)),
        compiler_params=params(16),
    )(currents, base, tail_before, block_inverses)


def solution(mesh):
    in_specs = (
        P("clus", "tm", None),
        P("clus", "tm", None),
        P("clus", None),
        P(),
        P(),
        P("clus", None, None),
        P(),
        P(),
    )
    out_specs = (P("clus", "tm", None), P("clus", "tm", None))
    return jax.shard_map(
        on_device, mesh=mesh, in_specs=in_specs, out_specs=out_specs, check_vma=False
    )
```

```python
import functools

import jax
import jax.numpy as jnp
from jax import lax
from jax.experimental import pallas as pl
from jax.experimental.pallas import tpu as pltpu
from jax.sharding import PartitionSpec as P

F32, BF16 = jnp.float32, jnp.bfloat16
MIB = 1 << 20


def whole(space=pltpu.VMEM):
    return pl.BlockSpec(memory_space=space)


def dot(a, b):
    return jnp.dot(a, b, preferred_element_type=F32)


def prep_kernel(cur_ref, map_ref, running_ref, totals_ref):
    per_dev, steps, unknowns = cur_ref.shape
    row = lax.broadcasted_iota(jnp.int32, (steps, 2 * steps), 0)
    col = lax.broadcasted_iota(jnp.int32, (steps, 2 * steps), 1)
    lower = (row >= col % steps).astype(F32).astype(BF16)
    group = 8

    @pl.loop(0, per_dev // group)
    def _(g):
        first = g * group
        rows = cur_ref[pl.ds(first, group)].reshape(group * steps, unknowns)
        inc = dot(rows, map_ref[...])
        high = inc.astype(BF16)
        low = (inc - high.astype(F32)).astype(BF16)
        last = []
        for i in range(group):
            cut = slice(i * steps, (i + 1) * steps)
            run = dot(lower, jnp.concatenate([high[cut], low[cut]], axis=0))
            running_ref[first + i] = run
            last.append(run[steps - 1 : steps])
        totals = jnp.concatenate(last, axis=0)
        for t in range(totals_ref.shape[0]):
            totals_ref[t, pl.ds(first, group)] = totals


def layout_kernel(lag_ref, own_ref, inner_ref, outer_ref, field_ref, toep_ref):
    per_dev, steps, unknowns = own_ref.shape
    slots = lag_ref.shape[0]
    lane = lax.broadcasted_iota(jnp.int32, (2 * steps, 2 * steps), 1)
    for p in range(slots // 2):
        even = jnp.broadcast_to(lag_ref[2 * p : 2 * p + 1, :], lane.shape)
        odd = jnp.broadcast_to(lag_ref[2 * p + 1 : 2 * p + 2, :], lane.shape)
        even = pltpu.roll(even, 0, 1, stride=1, stride_axis=0)
        odd = pltpu.roll(odd, steps, 1, stride=1, stride_axis=0)
        both = jnp.where(lane < steps, even, odd)
        toep_ref[:, p * 2 * steps : (p + 1) * 2 * steps] = both.astype(BF16)
    for part, ref in enumerate((own_ref, inner_ref, outer_ref)):
        field_ref[part * per_dev : (part + 1) * per_dev] = ref[...]
    field_ref[3 * per_dev] = jnp.zeros((steps, unknowns), BF16)


def near_kernel(
    start, ids_ref, field, coup_ref, toep_ref, head_ref, tail_ref, terms,
):
    count, steps, unknowns = head_ref.shape
    slots = coup_ref.shape[0]
    group = min(16, count)

    @pl.loop(0, count // group)
    def _(g):
        first = g * group
        for k in range(slots):
            rows = [field[ids_ref[start + first + i, k]] for i in range(group)]
            z = dot(jnp.concatenate(rows, axis=0), coup_ref[k]).astype(BF16)
            at = slice(k * steps, (k + 1) * steps)
            for i in range(group):
                lanes = slice((i % 2) * unknowns, (i % 2 + 1) * unknowns)
                terms[i // 2, at, lanes] = z[i * steps : (i + 1) * steps]
        for i in range(0, group, 2):
            out = dot(toep_ref[...], terms[i // 2])
            for j in range(2):
                lanes = slice(j * unknowns, (j + 1) * unknowns)
                head_ref[first + i + j] = out[:steps, lanes]
                tail_ref[first + i + j] = out[steps:, lanes].astype(BF16)


def base_kernel(exc_ref, low_ref, high_ref, running_ref, before_ref, pot_ref, base_ref):
    per_dev, steps, unknowns = exc_ref.shape
    group = per_dev // 4
    for g in range(4):
        at = slice(g * group, (g + 1) * group)
        head = (low_ref, high_ref)[g // 2][g % 2 * group : (g % 2 + 1) * group]
        charge = (running_ref[at] + before_ref[at][:, None, :]).astype(BF16)
        field = dot(charge.reshape(group * steps, -1), pot_ref[...])
        field = field.reshape(group, steps, unknowns)
        base_ref[at] = exc_ref[at].astype(F32) - head - field


def final_kernel(cur_ref, base_ref, tail_ref, inv_ref, *refs):
    updated_ref, residual_ref = refs[-2:]
    for i in range(cur_ref.shape[0]):
        residual = base_ref[i] - tail_ref[i].astype(F32)
        residual_ref[i] = residual
        correction = dot(residual.astype(BF16), inv_ref[i])
        updated_ref[i] = (cur_ref[i].astype(F32) + correction).astype(BF16)


def on_device(
    currents, excitation, neighbours, lag_profile, couplings, block_inverses, charge_map, potential
):
    per_dev, steps, unknowns = currents.shape
    slots, lags = lag_profile.shape
    blocks, peers = lax.axis_size("tm"), lax.axis_size("clus")
    me = lax.axis_index("clus")

    def send(x, where):
        pairs = [
            (t * peers + c, u * peers + d % peers)
            for t in range(blocks)
            for c in range(peers)
            for u, d in [where(t, c)]
            if 0 <= u < blocks
        ]
        return lax.ppermute(x, ("tm", "clus"), pairs)

    def behind(x, by):
        return send(x, lambda t, c: (t + by, c))

    outer = send(currents, lambda t, c: (t, c + 1 if c % 2 else c - 1))
    inner = send(currents, lambda t, c: (t, c ^ 1))
    shape3 = (per_dev, steps, unknowns)
    sds = jax.ShapeDtypeStruct
    params = lambda mib: pltpu.CompilerParams(vmem_limit_bytes=mib * MIB)
    lag_rows = jnp.pad(lag_profile.astype(F32), ((0, 0), (0, 2 * steps - lags)))
    lag_rows = jnp.roll(lag_rows[:, ::-1], 1, axis=1)
    running, totals = pl.pallas_call(
        prep_kernel,
        name="prep",
        out_shape=(
            sds(shape3, F32),
            sds((blocks, per_dev, unknowns), F32),
        ),
        in_specs=[whole()] * 2,
        out_specs=(whole(),) * 2,
        compiler_params=params(16),
    )(currents, charge_map)

    owner = neighbours // per_dev
    part = jnp.where(owner == me, 0, jnp.where(owner == me ^ 1, 1, 2))
    ids = jnp.where(neighbours >= 0, part * per_dev + neighbours % per_dev, 3 * per_dev)

    lag_rows, running = lax.optimization_barrier((lag_rows, running))
    pieces = lax.all_to_all(totals, "tm", 0, 0)
    field, toeplitz = pl.pallas_call(
        layout_kernel,
        name="layout",
        out_shape=(
            sds((3 * per_dev + 1, steps, unknowns), BF16),
            sds((2 * steps, slots * steps), BF16),
        ),
        in_specs=[whole()] * 4,
        out_specs=(whole(), whole()),
        compiler_params=params(16),
    )(lag_rows, currents, inner, outer)
    part = per_dev // 2
    heads, tails = [], []
    for h in range(2):
        head, tail = pl.pallas_call(
            functools.partial(near_kernel, h * part),
            name="near",
            out_shape=(sds((part, steps, unknowns), F32), sds((part, steps, unknowns), BF16)),
            in_specs=[whole(pltpu.SMEM)] + [whole()] * 3,
            out_specs=(whole(), whole()),
            scratch_shapes=[pltpu.VMEM((8, slots * steps, 2 * unknowns), BF16)],
            compiler_params=params(24),
            cost_estimate=pl.CostEstimate(
                flops=2 * part * slots * steps * unknowns * (unknowns + 2 * steps),
                bytes_accessed=4 * MIB,
                transcendentals=0,
            ),
        )(ids, field, couplings, toeplitz)
        ids, head = lax.optimization_barrier((ids, head))
        heads.append(head)
        tails.append(behind(tail, 1))
    earlier = jnp.arange(blocks) < lax.axis_index("tm")
    pieces, heads[1] = lax.optimization_barrier((pieces, heads[1]))
    before = jnp.sum(jnp.where(earlier[:, None, None], pieces, 0.0), axis=0)
    base = pl.pallas_call(
        base_kernel,
        name="base",
        out_shape=sds(shape3, F32),
        in_specs=[whole()] * 6,
        out_specs=whole(),
        compiler_params=params(16),
    )(excitation, *heads, running, before, potential)
    done = ()
    for h in range(2):
        at = lambda i, h=h: (h, 0, 0)
        mine = pl.BlockSpec((part, steps, unknowns), at)
        done = pl.pallas_call(
            final_kernel,
            name="final",
            grid=(1,),
            out_shape=(sds(shape3, BF16), sds(shape3, F32)),
            in_specs=[mine, mine, whole(), pl.BlockSpec((part, unknowns, unknowns), at)]
            + [whole(pl.ANY)] * len(done),
            out_specs=(mine, mine),
            input_output_aliases={4: 0, 5: 1} if done else {},
            compiler_params=params(16),
        )(currents, base, tails[h], block_inverses, *done)
    return done


def solution(mesh):
    in_specs = (
        P("clus", "tm", None),
        P("clus", "tm", None),
        P("clus", None),
        P(),
        P(),
        P("clus", None, None),
        P(),
        P(),
    )
    out_specs = (P("clus", "tm", None), P("clus", "tm", None))
    return jax.shard_map(
        on_device, mesh=mesh, in_specs=in_specs, out_specs=out_specs, check_vma=False
    )
```

```python
import functools

import jax
import jax.numpy as jnp
from jax import lax
from jax.experimental import pallas as pl
from jax.experimental.pallas import tpu as pltpu
from jax.sharding import PartitionSpec as P

F32, BF16 = jnp.float32, jnp.bfloat16
MIB = 1 << 20


def whole(space=pltpu.VMEM):
    return pl.BlockSpec(memory_space=space)


def dot(a, b):
    return jnp.dot(a, b, preferred_element_type=F32)


def prep_kernel(cur_ref, map_ref, running_ref, totals_ref):
    per_dev, steps, unknowns = cur_ref.shape
    row = lax.broadcasted_iota(jnp.int32, (steps, 2 * steps), 0)
    col = lax.broadcasted_iota(jnp.int32, (steps, 2 * steps), 1)
    lower = (row >= col % steps).astype(F32).astype(BF16)
    group = 8

    @pl.loop(0, per_dev // group)
    def _(g):
        first = g * group
        rows = cur_ref[pl.ds(first, group)].reshape(group * steps, unknowns)
        inc = dot(rows, map_ref[...])
        high = inc.astype(BF16)
        low = (inc - high.astype(F32)).astype(BF16)
        last = []
        for i in range(group):
            cut = slice(i * steps, (i + 1) * steps)
            run = dot(lower, jnp.concatenate([high[cut], low[cut]], axis=0))
            running_ref[first + i] = run
            last.append(run[steps - 1 : steps])
        totals = jnp.concatenate(last, axis=0)
        for t in range(totals_ref.shape[0]):
            totals_ref[t, pl.ds(first, group)] = totals


def layout_kernel(lag_ref, own_ref, inner_ref, outer_ref, field_ref, toep_ref):
    per_dev, steps, unknowns = own_ref.shape
    slots = lag_ref.shape[0]
    lane = lax.broadcasted_iota(jnp.int32, (2 * steps, 2 * steps), 1)
    for p in range(slots // 2):
        even = jnp.broadcast_to(lag_ref[2 * p : 2 * p + 1, :], lane.shape)
        odd = jnp.broadcast_to(lag_ref[2 * p + 1 : 2 * p + 2, :], lane.shape)
        even = pltpu.roll(even, 0, 1, stride=1, stride_axis=0)
        odd = pltpu.roll(odd, steps, 1, stride=1, stride_axis=0)
        both = jnp.where(lane < steps, even, odd)
        toep_ref[:, p * 2 * steps : (p + 1) * 2 * steps] = both.astype(BF16)
    for part, ref in enumerate((own_ref, inner_ref, outer_ref)):
        field_ref[part * per_dev : (part + 1) * per_dev] = ref[...]
    field_ref[3 * per_dev] = jnp.zeros((steps, unknowns), BF16)


def near_kernel(
    start, ids_ref, field, coup_ref, toep_ref, head_ref, tail_ref, terms,
):
    count, steps, unknowns = head_ref.shape
    slots = coup_ref.shape[0]
    group = min(8, count)

    @pl.loop(0, count // group)
    def _(g):
        first = g * group
        for k in range(slots):
            rows = [field[ids_ref[start + first + i, k]] for i in range(group)]
            z = dot(jnp.concatenate(rows, axis=0), coup_ref[k]).astype(BF16)
            at = slice(k * steps, (k + 1) * steps)
            for i in range(group):
                lanes = slice((i % 2) * unknowns, (i % 2 + 1) * unknowns)
                terms[i // 2, at, lanes] = z[i * steps : (i + 1) * steps]
        for i in range(0, group, 2):
            out = dot(toep_ref[...], terms[i // 2])
            for j in range(2):
                lanes = slice(j * unknowns, (j + 1) * unknowns)
                head_ref[first + i + j] = out[:steps, lanes]
                tail_ref[first + i + j] = out[steps:, lanes].astype(BF16)


def base_kernel(exc_ref, low_ref, high_ref, running_ref, before_ref, pot_ref, base_ref):
    per_dev, steps, unknowns = exc_ref.shape
    group = per_dev // 4
    for g in range(4):
        at = slice(g * group, (g + 1) * group)
        head = (low_ref, high_ref)[g // 2][g % 2 * group : (g % 2 + 1) * group]
        charge = (running_ref[at] + before_ref[at][:, None, :]).astype(BF16)
        field = dot(charge.reshape(group * steps, -1), pot_ref[...])
        field = field.reshape(group, steps, unknowns)
        base_ref[at] = exc_ref[at].astype(F32) - head - field


def final_kernel(cur_ref, base_ref, tail_ref, inv_ref, *refs):
    updated_ref, residual_ref = refs[-2:]
    for i in range(cur_ref.shape[0]):
        residual = base_ref[i] - tail_ref[i].astype(F32)
        residual_ref[i] = residual
        correction = dot(residual.astype(BF16), inv_ref[i])
        updated_ref[i] = (cur_ref[i].astype(F32) + correction).astype(BF16)


def on_device(
    currents, excitation, neighbours, lag_profile, couplings, block_inverses, charge_map, potential
):
    per_dev, steps, unknowns = currents.shape
    slots, lags = lag_profile.shape
    blocks, peers = lax.axis_size("tm"), lax.axis_size("clus")
    me = lax.axis_index("clus")

    def send(x, where):
        pairs = [
            (t * peers + c, u * peers + d % peers)
            for t in range(blocks)
            for c in range(peers)
            for u, d in [where(t, c)]
            if 0 <= u < blocks
        ]
        return lax.ppermute(x, ("tm", "clus"), pairs)

    def behind(x, by):
        return send(x, lambda t, c: (t + by, c))

    outer = send(currents, lambda t, c: (t, c + 1 if c % 2 else c - 1))
    inner = send(currents, lambda t, c: (t, c ^ 1))
    shape3 = (per_dev, steps, unknowns)
    sds = jax.ShapeDtypeStruct
    params = lambda mib: pltpu.CompilerParams(vmem_limit_bytes=mib * MIB)
    lag_rows = jnp.pad(lag_profile.astype(F32), ((0, 0), (0, 2 * steps - lags)))
    lag_rows = jnp.roll(lag_rows[:, ::-1], 1, axis=1)
    running, totals = pl.pallas_call(
        prep_kernel,
        name="prep",
        out_shape=(
            sds(shape3, F32),
            sds((blocks, per_dev, unknowns), F32),
        ),
        in_specs=[whole()] * 2,
        out_specs=(whole(),) * 2,
        compiler_params=params(16),
    )(currents, charge_map)

    owner = neighbours // per_dev
    part = jnp.where(owner == me, 0, jnp.where(owner == me ^ 1, 1, 2))
    ids = jnp.where(neighbours >= 0, part * per_dev + neighbours % per_dev, 3 * per_dev)

    lag_rows, running = lax.optimization_barrier((lag_rows, running))
    pieces = lax.all_to_all(totals, "tm", 0, 0)
    field, toeplitz = pl.pallas_call(
        layout_kernel,
        name="layout",
        out_shape=(
            sds((3 * per_dev + 1, steps, unknowns), BF16),
            sds((2 * steps, slots * steps), BF16),
        ),
        in_specs=[whole()] * 4,
        out_specs=(whole(), whole()),
        compiler_params=params(16),
    )(lag_rows, currents, inner, outer)
    part = per_dev // 2
    heads, tails = [], []
    for h in range(2):
        head, tail = pl.pallas_call(
            functools.partial(near_kernel, h * part),
            name="near",
            out_shape=(sds((part, steps, unknowns), F32), sds((part, steps, unknowns), BF16)),
            in_specs=[whole(pltpu.SMEM)] + [whole()] * 3,
            out_specs=(whole(), whole()),
            scratch_shapes=[pltpu.VMEM((4, slots * steps, 2 * unknowns), BF16)],
            compiler_params=params(24),
            cost_estimate=pl.CostEstimate(
                flops=2 * part * slots * steps * unknowns * (unknowns + 2 * steps),
                bytes_accessed=4 * MIB,
                transcendentals=0,
            ),
        )(ids, field, couplings, toeplitz)
        ids, head = lax.optimization_barrier((ids, head))
        heads.append(head)
        tails.append(behind(tail, 1))
    earlier = jnp.arange(blocks) < lax.axis_index("tm")
    pieces, heads[1] = lax.optimization_barrier((pieces, heads[1]))
    before = jnp.sum(jnp.where(earlier[:, None, None], pieces, 0.0), axis=0)
    base = pl.pallas_call(
        base_kernel,
        name="base",
        out_shape=sds(shape3, F32),
        in_specs=[whole()] * 6,
        out_specs=whole(),
        compiler_params=params(16),
    )(excitation, *heads, running, before, potential)
    done = ()
    for h in range(2):
        at = lambda i, h=h: (h, 0, 0)
        mine = pl.BlockSpec((part, steps, unknowns), at)
        done = pl.pallas_call(
            final_kernel,
            name="final",
            grid=(1,),
            out_shape=(sds(shape3, BF16), sds(shape3, F32)),
            in_specs=[mine, mine, whole(), pl.BlockSpec((part, unknowns, unknowns), at)]
            + [whole(pl.ANY)] * len(done),
            out_specs=(mine, mine),
            input_output_aliases={4: 0, 5: 1} if done else {},
            compiler_params=params(16),
        )(currents, base, tails[h], block_inverses, *done)
    return done


def solution(mesh):
    in_specs = (
        P("clus", "tm", None),
        P("clus", "tm", None),
        P("clus", None),
        P(),
        P(),
        P("clus", None, None),
        P(),
        P(),
    )
    out_specs = (P("clus", "tm", None), P("clus", "tm", None))
    return jax.shard_map(
        on_device, mesh=mesh, in_specs=in_specs, out_specs=out_specs, check_vma=False
    )
```

```python
import functools

import jax
import jax.numpy as jnp
from jax import lax
from jax.experimental import pallas as pl
from jax.experimental.pallas import tpu as pltpu
from jax.sharding import PartitionSpec as P

F32, BF16 = jnp.float32, jnp.bfloat16
MIB = 1 << 20


def whole(space=pltpu.VMEM):
    return pl.BlockSpec(memory_space=space)


def dot(a, b):
    return jnp.dot(a, b, preferred_element_type=F32)


def prep_kernel(cur_ref, map_ref, running_ref, totals_ref):
    per_dev, steps, unknowns = cur_ref.shape
    row = lax.broadcasted_iota(jnp.int32, (steps, 2 * steps), 0)
    col = lax.broadcasted_iota(jnp.int32, (steps, 2 * steps), 1)
    lower = (row >= col % steps).astype(F32).astype(BF16)
    group = 8

    @pl.loop(0, per_dev // group)
    def _(g):
        first = g * group
        rows = cur_ref[pl.ds(first, group)].reshape(group * steps, unknowns)
        inc = dot(rows, map_ref[...])
        high = inc.astype(BF16)
        low = (inc - high.astype(F32)).astype(BF16)
        last = []
        for i in range(group):
            cut = slice(i * steps, (i + 1) * steps)
            run = dot(lower, jnp.concatenate([high[cut], low[cut]], axis=0))
            running_ref[first + i] = run
            last.append(run[steps - 1 : steps])
        totals = jnp.concatenate(last, axis=0)
        for t in range(totals_ref.shape[0]):
            totals_ref[t, pl.ds(first, group)] = totals


def layout_kernel(lag_ref, own_ref, inner_ref, outer_ref, field_ref, toep_ref):
    per_dev, steps, unknowns = own_ref.shape
    slots = lag_ref.shape[0]
    lane = lax.broadcasted_iota(jnp.int32, (2 * steps, 2 * steps), 1)
    for p in range(slots // 2):
        even = jnp.broadcast_to(lag_ref[2 * p : 2 * p + 1, :], lane.shape)
        odd = jnp.broadcast_to(lag_ref[2 * p + 1 : 2 * p + 2, :], lane.shape)
        even = pltpu.roll(even, 0, 1, stride=1, stride_axis=0)
        odd = pltpu.roll(odd, steps, 1, stride=1, stride_axis=0)
        both = jnp.where(lane < steps, even, odd)
        toep_ref[:, p * 2 * steps : (p + 1) * 2 * steps] = both.astype(BF16)
    for part, ref in enumerate((own_ref, inner_ref, outer_ref)):
        field_ref[part * per_dev : (part + 1) * per_dev] = ref[...]
    field_ref[3 * per_dev] = jnp.zeros((steps, unknowns), BF16)


def near_kernel(
    start, ids_ref, field, coup_ref, toep_ref, head_ref, tail_ref, terms,
):
    count, steps, unknowns = head_ref.shape
    slots = coup_ref.shape[0]
    group = min(8, count)

    @pl.loop(0, count // group)
    def _(g):
        first = g * group
        for k in range(slots):
            rows = [field[ids_ref[start + first + i, k]] for i in range(group)]
            z = dot(jnp.concatenate(rows, axis=0), coup_ref[k]).astype(BF16)
            at = slice(k * steps, (k + 1) * steps)
            for i in range(group):
                lanes = slice((i % 2) * unknowns, (i % 2 + 1) * unknowns)
                terms[i // 2, at, lanes] = z[i * steps : (i + 1) * steps]
        for i in range(0, group, 2):
            out = dot(toep_ref[...], terms[i // 2])
            for j in range(2):
                lanes = slice(j * unknowns, (j + 1) * unknowns)
                head_ref[first + i + j] = out[:steps, lanes]
                tail_ref[first + i + j] = out[steps:, lanes].astype(BF16)


def base_kernel(block_ref, exc_ref, low_ref, high_ref, running_ref, pieces_ref, pot_ref, base_ref):
    per_dev, steps, unknowns = exc_ref.shape
    before = jnp.zeros(pieces_ref.shape[1:], F32)
    for t in range(pieces_ref.shape[0] - 1):
        before += jnp.where(t < block_ref[0], pieces_ref[t], 0.0)
    group = per_dev // 4
    for g in range(4):
        at = slice(g * group, (g + 1) * group)
        head = low_ref[at] if g < 3 else high_ref[...]
        charge = (running_ref[at] + before[at][:, None, :]).astype(BF16)
        field = dot(charge.reshape(group * steps, -1), pot_ref[...])
        field = field.reshape(group, steps, unknowns)
        base_ref[at] = exc_ref[at].astype(F32) - head - field


def final_kernel(cur_ref, base_ref, tail_ref, inv_ref, *refs):
    updated_ref, residual_ref = refs[-2:]
    for i in range(cur_ref.shape[0]):
        residual = base_ref[i] - tail_ref[i].astype(F32)
        residual_ref[i] = residual
        correction = dot(residual.astype(BF16), inv_ref[i])
        updated_ref[i] = (cur_ref[i].astype(F32) + correction).astype(BF16)


def on_device(
    currents, excitation, neighbours, lag_profile, couplings, block_inverses, charge_map, potential
):
    per_dev, steps, unknowns = currents.shape
    slots, lags = lag_profile.shape
    blocks, peers = lax.axis_size("tm"), lax.axis_size("clus")
    me = lax.axis_index("clus")

    def send(x, where):
        pairs = [
            (t * peers + c, u * peers + d % peers)
            for t in range(blocks)
            for c in range(peers)
            for u, d in [where(t, c)]
            if 0 <= u < blocks
        ]
        return lax.ppermute(x, ("tm", "clus"), pairs)

    def behind(x, by):
        return send(x, lambda t, c: (t + by, c))

    outer = send(currents, lambda t, c: (t, c + 1 if c % 2 else c - 1))
    inner = send(currents, lambda t, c: (t, c ^ 1))
    shape3 = (per_dev, steps, unknowns)
    sds = jax.ShapeDtypeStruct
    params = lambda mib: pltpu.CompilerParams(vmem_limit_bytes=mib * MIB)
    lag_rows = jnp.pad(lag_profile.astype(F32), ((0, 0), (0, 2 * steps - lags)))
    lag_rows = jnp.roll(lag_rows[:, ::-1], 1, axis=1)
    running, totals = pl.pallas_call(
        prep_kernel,
        name="prep",
        out_shape=(
            sds(shape3, F32),
            sds((blocks, per_dev, unknowns), F32),
        ),
        in_specs=[whole()] * 2,
        out_specs=(whole(),) * 2,
        compiler_params=params(16),
    )(currents, charge_map)

    owner = neighbours // per_dev
    part = jnp.where(owner == me, 0, jnp.where(owner == me ^ 1, 1, 2))
    ids = jnp.where(neighbours >= 0, part * per_dev + neighbours % per_dev, 3 * per_dev)

    lag_rows, running = lax.optimization_barrier((lag_rows, running))
    pieces = lax.all_to_all(totals, "tm", 0, 0)
    field, toeplitz = pl.pallas_call(
        layout_kernel,
        name="layout",
        out_shape=(
            sds((3 * per_dev + 1, steps, unknowns), BF16),
            sds((2 * steps, slots * steps), BF16),
        ),
        in_specs=[whole()] * 4,
        out_specs=(whole(), whole()),
        compiler_params=params(16),
    )(lag_rows, currents, inner, outer)
    most = 3 * per_dev // 4
    cuts = ((0, most), (most, per_dev - most))
    heads, tails = [], []
    for first, part in cuts:
        head, tail = pl.pallas_call(
            functools.partial(near_kernel, first),
            name="near",
            out_shape=(sds((part, steps, unknowns), F32), sds((part, steps, unknowns), BF16)),
            in_specs=[whole(pltpu.SMEM)] + [whole()] * 3,
            out_specs=(whole(), whole()),
            scratch_shapes=[pltpu.VMEM((4, slots * steps, 2 * unknowns), BF16)],
            compiler_params=params(24),
            cost_estimate=pl.CostEstimate(
                flops=2 * part * slots * steps * unknowns * (unknowns + 2 * steps),
                bytes_accessed=4 * MIB,
                transcendentals=0,
            ),
        )(ids, field, couplings, toeplitz)
        ids, head = lax.optimization_barrier((ids, head))
        heads.append(head)
        tails.append(behind(tail, 1))
    mine = lax.axis_index("tm").astype(jnp.int32).reshape(1)
    pieces, heads[1] = lax.optimization_barrier((pieces, heads[1]))
    base = pl.pallas_call(
        base_kernel,
        name="base",
        out_shape=sds(shape3, F32),
        in_specs=[whole(pltpu.SMEM)] + [whole()] * 6,
        out_specs=whole(),
        compiler_params=params(16),
    )(mine, excitation, *heads, running, pieces, potential)
    done = ()
    for tail, (first, part) in zip(tails, cuts):
        at = lambda i, n=first // part: (n, 0, 0)
        block = pl.BlockSpec((part, steps, unknowns), at)
        done = pl.pallas_call(
            final_kernel,
            name="final",
            grid=(1,),
            out_shape=(sds(shape3, BF16), sds(shape3, F32)),
            in_specs=[block, block, whole(), pl.BlockSpec((part, unknowns, unknowns), at)]
            + [whole(pl.ANY)] * len(done),
            out_specs=(block, block),
            input_output_aliases={4: 0, 5: 1} if done else {},
            compiler_params=params(16),
        )(currents, base, tail, block_inverses, *done)
    return done


def solution(mesh):
    in_specs = (
        P("clus", "tm", None),
        P("clus", "tm", None),
        P("clus", None),
        P(),
        P(),
        P("clus", None, None),
        P(),
        P(),
    )
    out_specs = (P("clus", "tm", None), P("clus", "tm", None))
    return jax.shard_map(
        on_device, mesh=mesh, in_specs=in_specs, out_specs=out_specs, check_vma=False
    )
```

```python
import functools

import jax
import jax.numpy as jnp
from jax import lax
from jax.experimental import pallas as pl
from jax.experimental.pallas import tpu as pltpu
from jax.sharding import PartitionSpec as P

F32, BF16 = jnp.float32, jnp.bfloat16
MIB = 1 << 20


def whole(space=pltpu.VMEM):
    return pl.BlockSpec(memory_space=space)


def dot(a, b):
    return jnp.dot(a, b, preferred_element_type=F32)


def prep_kernel(cur_ref, map_ref, running_ref, totals_ref):
    per_dev, steps, unknowns = cur_ref.shape
    row = lax.broadcasted_iota(jnp.int32, (steps, 2 * steps), 0)
    col = lax.broadcasted_iota(jnp.int32, (steps, 2 * steps), 1)
    lower = (row >= col % steps).astype(F32).astype(BF16)
    group = 8

    @pl.loop(0, per_dev // group)
    def _(g):
        first = g * group
        rows = cur_ref[pl.ds(first, group)].reshape(group * steps, unknowns)
        inc = dot(rows, map_ref[...])
        high = inc.astype(BF16)
        low = (inc - high.astype(F32)).astype(BF16)
        last = []
        for i in range(group):
            cut = slice(i * steps, (i + 1) * steps)
            run = dot(lower, jnp.concatenate([high[cut], low[cut]], axis=0))
            running_ref[first + i] = run
            last.append(run[steps - 1 : steps])
        totals = jnp.concatenate(last, axis=0)
        for t in range(totals_ref.shape[0]):
            totals_ref[t, pl.ds(first, group)] = totals


def layout_kernel(
    me_ref, near_ref, lag_ref, own_ref, inner_ref, outer_ref, ids_ref, field_ref, toep_ref,
):
    per_dev, steps, unknowns = own_ref.shape
    slots, lags = lag_ref.shape
    wide = 2 * steps
    source = lax.broadcasted_iota(jnp.int32, (lags, wide), 0)
    target = lax.broadcasted_iota(jnp.int32, (lags, wide), 1)
    flip = ((source + target) % wide == 0).astype(F32).astype(BF16)
    lag_rows = dot(lag_ref[...], flip)
    owner = near_ref[...] // per_dev
    part = jnp.where(owner == me_ref[0], 0, jnp.where(owner == me_ref[0] ^ 1, 1, 2))
    inside = part * per_dev + near_ref[...] % per_dev
    ids_ref[...] = jnp.where(near_ref[...] >= 0, inside, 3 * per_dev)
    lane = lax.broadcasted_iota(jnp.int32, (2 * steps, 2 * steps), 1)
    for p in range(slots // 2):
        even = jnp.broadcast_to(lag_rows[2 * p : 2 * p + 1, :], lane.shape)
        odd = jnp.broadcast_to(lag_rows[2 * p + 1 : 2 * p + 2, :], lane.shape)
        even = pltpu.roll(even, 0, 1, stride=1, stride_axis=0)
        odd = pltpu.roll(odd, steps, 1, stride=1, stride_axis=0)
        both = jnp.where(lane < steps, even, odd)
        toep_ref[:, p * 2 * steps : (p + 1) * 2 * steps] = both.astype(BF16)
    for part, ref in enumerate((own_ref, inner_ref, outer_ref)):
        field_ref[part * per_dev : (part + 1) * per_dev] = ref[...]
    field_ref[3 * per_dev] = jnp.zeros((steps, unknowns), BF16)


def near_kernel(
    start, ids_ref, field, coup_ref, toep_ref, head_ref, tail_ref, terms,
):
    count, steps, unknowns = head_ref.shape
    slots = coup_ref.shape[0]
    group = min(16, count)

    @pl.loop(0, count // group)
    def _(g):
        first = g * group
        for k in range(slots):
            rows = [field[ids_ref[start + first + i, k]] for i in range(group)]
            z = dot(jnp.concatenate(rows, axis=0), coup_ref[k]).astype(BF16)
            at = slice(k * steps, (k + 1) * steps)
            for i in range(group):
                lanes = slice((i % 2) * unknowns, (i % 2 + 1) * unknowns)
                terms[i // 2, at, lanes] = z[i * steps : (i + 1) * steps]
        for i in range(0, group, 2):
            out = dot(toep_ref[...], terms[i // 2])
            for j in range(2):
                lanes = slice(j * unknowns, (j + 1) * unknowns)
                head_ref[first + i + j] = out[:steps, lanes]
                tail_ref[first + i + j] = out[steps:, lanes].astype(BF16)


def base_kernel(exc_ref, low_ref, high_ref, running_ref, before_ref, pot_ref, base_ref):
    per_dev, steps, unknowns = exc_ref.shape
    group = per_dev // 4
    for g in range(4):
        at = slice(g * group, (g + 1) * group)
        head = (low_ref, high_ref)[g // 2][g % 2 * group : (g % 2 + 1) * group]
        charge = (running_ref[at] + before_ref[at][:, None, :]).astype(BF16)
        field = dot(charge.reshape(group * steps, -1), pot_ref[...])
        field = field.reshape(group, steps, unknowns)
        base_ref[at] = exc_ref[at].astype(F32) - head - field


def final_kernel(cur_ref, base_ref, tail_ref, inv_ref, *refs):
    updated_ref, residual_ref = refs[-2:]
    for i in range(cur_ref.shape[0]):
        residual = base_ref[i] - tail_ref[i].astype(F32)
        residual_ref[i] = residual
        correction = dot(residual.astype(BF16), inv_ref[i])
        updated_ref[i] = (cur_ref[i].astype(F32) + correction).astype(BF16)


def on_device(
    currents, excitation, neighbours, lag_profile, couplings, block_inverses, charge_map, potential
):
    per_dev, steps, unknowns = currents.shape
    slots, lags = lag_profile.shape
    blocks, peers = lax.axis_size("tm"), lax.axis_size("clus")
    me = lax.axis_index("clus")

    def send(x, where):
        pairs = [
            (t * peers + c, u * peers + d % peers)
            for t in range(blocks)
            for c in range(peers)
            for u, d in [where(t, c)]
            if 0 <= u < blocks
        ]
        return lax.ppermute(x, ("tm", "clus"), pairs)

    def behind(x, by):
        return send(x, lambda t, c: (t + by, c))

    outer = send(currents, lambda t, c: (t, c + 1 if c % 2 else c - 1))
    inner = send(currents, lambda t, c: (t, c ^ 1))
    shape3 = (per_dev, steps, unknowns)
    sds = jax.ShapeDtypeStruct
    params = lambda mib: pltpu.CompilerParams(vmem_limit_bytes=mib * MIB)
    running, totals = pl.pallas_call(
        prep_kernel,
        name="prep",
        out_shape=(
            sds(shape3, F32),
            sds((blocks, per_dev, unknowns), F32),
        ),
        in_specs=[whole()] * 2,
        out_specs=(whole(),) * 2,
        compiler_params=params(16),
    )(currents, charge_map)

    pieces = lax.all_to_all(totals, "tm", 0, 0)
    ids, field, toeplitz = pl.pallas_call(
        layout_kernel,
        name="layout",
        out_shape=(
            sds(neighbours.shape, jnp.int32),
            sds((3 * per_dev + 1, steps, unknowns), BF16),
            sds((2 * steps, slots * steps), BF16),
        ),
        in_specs=[whole(pltpu.SMEM)] + [whole()] * 5,
        out_specs=(whole(),) * 3,
        compiler_params=params(16),
    )(me.astype(jnp.int32).reshape(1), neighbours, lag_profile, currents, inner, outer)
    part = per_dev // 2
    heads, tails = [], []
    for h in range(2):
        head, tail = pl.pallas_call(
            functools.partial(near_kernel, h * part),
            name="near",
            out_shape=(sds((part, steps, unknowns), F32), sds((part, steps, unknowns), BF16)),
            in_specs=[whole(pltpu.SMEM)] + [whole()] * 3,
            out_specs=(whole(), whole()),
            scratch_shapes=[pltpu.VMEM((8, slots * steps, 2 * unknowns), BF16)],
            compiler_params=params(24),
            cost_estimate=pl.CostEstimate(
                flops=2 * part * slots * steps * unknowns * (unknowns + 2 * steps),
                bytes_accessed=4 * MIB,
                transcendentals=0,
            ),
        )(ids, field, couplings, toeplitz)
        ids, head = lax.optimization_barrier((ids, head))
        heads.append(head)
        tails.append(behind(tail, 1))
    earlier = jnp.arange(blocks) < lax.axis_index("tm")
    pieces, heads[1] = lax.optimization_barrier((pieces, heads[1]))
    before = jnp.sum(jnp.where(earlier[:, None, None], pieces, 0.0), axis=0)
    base = pl.pallas_call(
        base_kernel,
        name="base",
        out_shape=sds(shape3, F32),
        in_specs=[whole()] * 6,
        out_specs=whole(),
        compiler_params=params(16),
    )(excitation, *heads, running, before, potential)
    done = ()
    for h in range(2):
        at = lambda i, h=h: (h, 0, 0)
        mine = pl.BlockSpec((part, steps, unknowns), at)
        done = pl.pallas_call(
            final_kernel,
            name="final",
            grid=(1,),
            out_shape=(sds(shape3, BF16), sds(shape3, F32)),
            in_specs=[mine, mine, whole(), pl.BlockSpec((part, unknowns, unknowns), at)]
            + [whole(pl.ANY)] * len(done),
            out_specs=(mine, mine),
            input_output_aliases={4: 0, 5: 1} if done else {},
            compiler_params=params(16),
        )(currents, base, tails[h], block_inverses, *done)
    return done


def solution(mesh):
    in_specs = (
        P("clus", "tm", None),
        P("clus", "tm", None),
        P("clus", None),
        P(),
        P(),
        P("clus", None, None),
        P(),
        P(),
    )
    out_specs = (P("clus", "tm", None), P("clus", "tm", None))
    return jax.shard_map(
        on_device, mesh=mesh, in_specs=in_specs, out_specs=out_specs, check_vma=False
    )
```
